128 devices in a mesh: group: 16 (over y, x), member: 8 (over z, core).
Axes of the slice: x: 4, y: 4, z: 4, core: 2. Of those that a mesh axis runs over, the one named last changes fastest.
Arguments:
- tokens: bfloat16 [16384, 2048], P(('group', 'member')), may hold values from -6 to 6
- grad_out: bfloat16 [16384, 2048], P(('group', 'member')), may hold values from -6 to 6
- expert_ids: int32 [16384, 8], P(('group', 'member')), may hold values from 0 to 127, as said below
- pair_slot: int32 [16384, 8], P(('group', 'member')), may hold values from 0 to 11, as said below
- gate_weights: bfloat16 [16384, 8], P(('group', 'member')), may hold values from 0.049804688 to 1
- weight_gate: bfloat16 [128, 2048, 768], P(('group', 'member')), may hold values from -0.125 to 0.125
- weight_up: bfloat16 [128, 2048, 768], P(('group', 'member')), may hold values from -0.125 to 0.125
- weight_down: bfloat16 [128, 768, 2048], P(('group', 'member')), may hold values from -0.21875 to 0.21875
- saved_gate: bfloat16 [128, 1536, 768], P(('group', 'member')), may hold values from -6 to 6
- saved_up: bfloat16 [128, 1536, 768], P(('group', 'member')), may hold values from -6 to 6
Outputs:
- grad_tokens: bfloat16 [16384, 2048], P(('group', 'member'))
- grad_gates: bfloat16 [16384, 8], P(('group', 'member'))
- grad_weight_gate: bfloat16 [128, 2048, 768], P(('group', 'member'))
- grad_weight_up: bfloat16 [128, 2048, 768], P(('group', 'member'))
- grad_weight_down: bfloat16 [128, 768, 2048], P(('group', 'member'))
The draws below stay inside these ranges and needn't reach their ends.
Inputs may be any that keep to these rules, and one draw needn't show every extreme that they name: `expert_ids`: each token names 8 distinct experts, two in each of exactly 4 groups, the group of expert e being e // 8. The tokens of one device send at most 48 tokens to one group, and in every draw some group gets exactly 48 from every device. `pair_slot`: among one device's assignments to one expert the slots are distinct and run from 0 to their count less one, in no fixed order of tokens. In every draw some expert gets exactly 12 assignments from every device.
All inputs are finite; a program needn't handle non-finite values.
Results may differ from the reference program's by a relative error of at most 0.012.
Values may be sent and summed in bfloat16 or wider, within the bound.
No kernel may reach another device: no remote copies, remote signals or barrier semaphores. Data moves between devices by JAX's collectives and lax.ppermute only.
A program may use at most 192 MiB of HBM per device.

```python
import math
import jax
import jax.numpy as jnp
from jax import lax

D = 2048
FF = 768
TOP = 8
GROUP_VISITS = 4
TOK_DEV = 128
GROUPS = 16
MEMBERS = 8
EXPERTS = 128
TOKENS = 16384
PAIR = 12
CAP = 1536
GROUP_SLOTS = 48


def routing_tables(key):
    base_key = jax.random.fold_in(key, 11)
    key_pop, key_hot, key_member, key_devices = jax.random.split(base_key, 4)
    expert_preference = jax.random.randint(key_pop, (GROUPS,), 0, 2048, dtype=jnp.int32)
    favored_group = jax.random.randint(key_hot, (), 0, GROUPS, dtype=jnp.int32)
    hot_member = jax.random.randint(key_member, (), 0, MEMBERS, dtype=jnp.int32)
    group_indices = jnp.arange(GROUPS, dtype=jnp.int32)
    member_range = jnp.arange(MEMBERS, dtype=jnp.int32)
    group_extra_score = expert_preference + jnp.where(group_indices == favored_group, 1 << 20, 0)

    def token_step(carry, token_key):
        group_total, expert_count = carry
        key_groups, key_experts = jax.random.split(token_key)
        group_jitter = jax.random.randint(key_groups, (GROUPS,), 0, 1024, dtype=jnp.int32)
        expert_noise = jax.random.randint(key_experts, (EXPERTS,), 0, 1024, dtype=jnp.int32)
        group_affinity = jnp.where(group_total < GROUP_SLOTS, group_extra_score + group_jitter - group_total * 1024, -(1 << 23)) * 64 + group_indices
        chosen_groups = lax.top_k(group_affinity, GROUP_VISITS)[1]
        chosen_experts = []
        chosen_slots = []
        for visit_number in range(GROUP_VISITS):
            group_pick = chosen_groups[visit_number]
            first_expert = group_pick * MEMBERS
            counts = lax.dynamic_slice(expert_count, (first_expert,), (MEMBERS,))
            noise_here = lax.dynamic_slice(expert_noise, (first_expert,), (MEMBERS,))
            hot_boost = jnp.where((group_pick == favored_group) & (member_range == hot_member), 1 << 22, 0)
            expert_score = jnp.where(counts < PAIR, noise_here - counts * 2048 + hot_boost, -(1 << 24)) * 64 + member_range
            picked = lax.top_k(expert_score, 2)[1]
            chosen_experts.append(first_expert + picked)
            chosen_slots.append(counts[picked])
            expert_count = expert_count.at[first_expert + picked].add(1)
            group_total = group_total.at[group_pick].add(1)
        return ((group_total, expert_count), (jnp.concatenate(chosen_experts), jnp.concatenate(chosen_slots)))

    def one_device(device_key):
        key_tokens, key_order = jax.random.split(device_key)
        start_carry = (jnp.zeros((GROUPS,), jnp.int32), jnp.zeros((EXPERTS,), jnp.int32))
        tables = lax.scan(token_step, start_carry, jax.random.split(key_tokens, TOK_DEV))[1]
        order = jax.random.permutation(key_order, TOK_DEV)
        return (tables[0][order], tables[1][order])
    experts_all, slots_all = jax.vmap(one_device)(jax.random.split(key_devices, EXPERTS))
    return (experts_all.reshape(TOKENS, TOP).astype(jnp.int32), slots_all.reshape(TOKENS, TOP).astype(jnp.int32))


def draw_expert_ids(key, part):
    return routing_tables(key)[0]


def draw_pair_slot(key, part):
    return routing_tables(key)[1]


def level_of(stream_key, shape, shards, low, top_value):
    def one(position, parts):
        steps = jax.random.uniform(jax.random.fold_in(jax.random.fold_in(stream_key, 6), position), (parts,), jnp.float32, low / len(shards), top_value / len(shards))
        return jnp.repeat(jnp.exp(steps), shape[position] // parts).reshape((-1,) + (1,) * (len(shape) - position - 1))

    gain = one(*shards[0])
    for cut in shards[1:]:
        gain = gain * one(*cut)
    return gain


def gaussian(stream_key, shape, deviation, reach, cuts=(), held_as=jnp.bfloat16):
    factor_of = level_of(stream_key, shape, cuts, -0.22, 0.18) if cuts else 1.0
    entries = jax.random.normal(stream_key, shape, jnp.float32) * deviation * factor_of
    return jnp.minimum(jnp.maximum(entries, -reach), reach).astype(held_as)


def setup_inputs(seed: int = 0) -> dict:
    key_of = jax.random.split(jax.random.key(seed), 11)
    tokens = gaussian(key_of[0], (TOKENS, D), 1.0, 6.0, ((0, 128),))
    grad_out = gaussian(key_of[1], (TOKENS, D), 1.0, 6.0, ((0, 128),))
    expert_ids = draw_expert_ids(jax.random.fold_in(key_of[10], 71), 0)
    pair_slot = draw_pair_slot(jax.random.fold_in(key_of[10], 71), 0)
    gate_weights = jnp.clip(jnp.exp(math.log(1.0) - 2.9996462 * jax.random.uniform(key_of[4], (TOKENS, TOP), jnp.float32) ** level_of(key_of[4], (TOKENS, TOP), ((0, 128),), -0.2, 0.2)), 0.049804688, 1.0).astype(jnp.bfloat16)
    weight_gate = gaussian(key_of[5], (EXPERTS, D, FF), D ** -0.5, 0.125, ((0, 128),))
    weight_up = gaussian(key_of[6], (EXPERTS, D, FF), D ** -0.5, 0.125, ((0, 128),))
    weight_down = gaussian(key_of[7], (EXPERTS, FF, D), FF ** -0.5, 0.21875, ((0, 128),))
    saved_gate = gaussian(key_of[8], (EXPERTS, CAP, FF), 1.0, 6.0, ((0, 128),))
    saved_up = gaussian(key_of[9], (EXPERTS, CAP, FF), 1.0, 6.0, ((0, 128),))
    return dict(tokens=tokens, grad_out=grad_out, expert_ids=expert_ids, pair_slot=pair_slot, gate_weights=gate_weights, weight_gate=weight_gate, weight_up=weight_up, weight_down=weight_down, saved_gate=saved_gate, saved_up=saved_up)


def expert_block(token_rows, grad_rows, route_gate, saved_pregate, saved_preup, weight_gate, weight_up, weight_down):
    pre_gate = saved_pregate.astype(jnp.float32)
    pre_up = saved_preup.astype(jnp.float32)
    gate_sigmoid = jax.nn.sigmoid(pre_gate)
    gate_swish = pre_gate * gate_sigmoid
    hidden = gate_swish * pre_up
    hidden_low = hidden.astype(jnp.bfloat16)
    route_scale = route_gate.astype(jnp.float32)[:, None]
    scaled_grads = (route_scale * grad_rows.astype(jnp.float32)).astype(jnp.bfloat16)
    down_grad = jnp.dot(hidden_low.T, scaled_grads, preferred_element_type=jnp.float32)
    back_hidden = jnp.dot(grad_rows, weight_down.T, preferred_element_type=jnp.float32)
    slot_gate = jnp.sum(hidden * back_hidden, axis=1).astype(jnp.bfloat16)
    hidden_grad = route_scale * back_hidden
    pregate_grad = (hidden_grad * pre_up * gate_sigmoid * (1.0 + pre_gate * (1.0 - gate_sigmoid))).astype(jnp.bfloat16)
    preup_grad = (hidden_grad * gate_swish).astype(jnp.bfloat16)
    gate_grad = jnp.dot(token_rows.T, pregate_grad, preferred_element_type=jnp.float32)
    up_grad = jnp.dot(token_rows.T, preup_grad, preferred_element_type=jnp.float32)
    slot_grad = (jnp.dot(pregate_grad, weight_gate.T, preferred_element_type=jnp.float32)
                 + jnp.dot(preup_grad, weight_up.T, preferred_element_type=jnp.float32)).astype(jnp.bfloat16)
    return slot_grad, slot_gate, gate_grad, up_grad, down_grad


def reference(tokens, grad_out, expert_ids, pair_slot, gate_weights, weight_gate, weight_up, weight_down, saved_gate, saved_up):
    route_total = TOKENS * TOP
    route_index = jnp.arange(route_total, dtype=jnp.int32)
    source = (route_index // TOP) // TOK_DEV
    flat_slot = (expert_ids.reshape(-1) * CAP + source * PAIR + pair_slot.reshape(-1)).astype(jnp.int32)
    slot_route = jnp.full((EXPERTS * CAP,), route_total, jnp.int32).at[flat_slot].set(route_index)
    gates_flat = gate_weights.reshape(-1)

    def expert_step(carry, expert):
        token_acc, term_acc = carry
        routes_here = lax.dynamic_slice(slot_route, (expert * CAP,), (CAP,))
        token_here = (routes_here // TOP).astype(jnp.int32)
        rows_here = jnp.take(tokens, token_here, axis=0, mode="fill", fill_value=0)
        grads_here = jnp.take(grad_out, token_here, axis=0, mode="fill", fill_value=0)
        gates_here = jnp.take(gates_flat, routes_here, axis=0, mode="fill", fill_value=0)
        slot_grad, slot_gate, gate_grad, up_grad, down_grad = expert_block(
            rows_here, grads_here, gates_here, saved_gate[expert], saved_up[expert],
            weight_gate[expert], weight_up[expert], weight_down[expert])
        token_acc = token_acc.at[token_here].add(slot_grad.astype(jnp.float32), mode="drop")
        term_acc = term_acc.at[routes_here].set(slot_gate.astype(jnp.float32), mode="drop")
        return (token_acc, term_acc), (gate_grad.astype(jnp.bfloat16), up_grad.astype(jnp.bfloat16), down_grad.astype(jnp.bfloat16))

    start_carry = (jnp.zeros((TOKENS, D), jnp.float32), jnp.zeros((route_total,), jnp.float32))
    final_carry, weight_grads = lax.scan(expert_step, start_carry, jnp.arange(EXPERTS, dtype=jnp.int32))
    token_acc, term_acc = final_carry
    return (token_acc.astype(jnp.bfloat16), term_acc.reshape(TOKENS, TOP).astype(jnp.bfloat16),
            weight_grads[0], weight_grads[1], weight_grads[2])
```

```python
import jax
import jax.numpy as jnp
from jax import lax
from jax.experimental import pallas as pl
from jax.experimental.pallas import tpu as pltpu
from jax.sharding import PartitionSpec as P

F32 = jnp.float32
BF16 = jnp.bfloat16
AXES = ("group", "member")
CHUNK = 256
NT = (((1,), (1,)), ((), ()))
VMEM_LIMIT = 56 * 1024 * 1024


def zero_one(mask):
    return jnp.where(mask, 1.0, 0.0).astype(BF16)


def dot(a, b):
    return jnp.dot(a, b, preferred_element_type=F32)


def packed_ids(index):
    pair, q = index >> 3, index & 7
    return pair * 12 + q, pair * 12 + 8 + (q & 3), q < 4


def pack_kernel(dest_ref, x_ref, out_ref):
    rows, toks = out_ref.shape[0], x_ref.shape[0]
    width = x_ref.shape[1]
    half = width // 2
    index = lax.broadcasted_iota(jnp.int32, (rows, toks), 0) + pl.program_id(0) * rows
    id_a, id_b, first = packed_ids(index)
    hit_a = dest_ref[0:1, :] == id_a
    hit_b = dest_ref[0:1, :] == id_b
    for k in range(1, dest_ref.shape[0]):
        d = dest_ref[k : k + 1, :]
        hit_a = hit_a | (d == id_a)
        hit_b = hit_b | (d == id_b)
    out_ref[:, :width] = dot(zero_one(hit_a), x_ref[...]).astype(BF16)
    low = dot(zero_one(hit_b & first), x_ref[:, :half])
    high = dot(zero_one(hit_b & jnp.logical_not(first)), x_ref[:, half:])
    out_ref[:, width:] = (low + high).astype(BF16)


def pack(dest_t, x, packed_rows):
    toks, width = x.shape
    return pl.pallas_call(
        pack_kernel,
        grid=(packed_rows // CHUNK,),
        in_specs=[
            pl.BlockSpec(dest_t.shape, lambda i: (0, 0)),
            pl.BlockSpec(x.shape, lambda i: (0, 0)),
        ],
        out_specs=pl.BlockSpec((CHUNK, width * 3 // 2), lambda i: (i, 0)),
        out_shape=jax.ShapeDtypeStruct((packed_rows, width * 3 // 2), BF16),
        compiler_params=pltpu.CompilerParams(vmem_limit_bytes=VMEM_LIMIT),
        cost_estimate=pl.CostEstimate(
            flops=2 * packed_rows * toks * width * 2,
            bytes_accessed=packed_rows * width * 3,
            transcendentals=0,
        ),
    )(dest_t, x)


def sort_kernel(a_ref, b_ref, out_a, out_b):
    rows = a_ref.shape[0]
    n = lax.broadcasted_iota(jnp.int32, (rows, rows), 0)
    col = lax.broadcasted_iota(jnp.int32, (rows, rows), 1)
    cut = rows * 2 // 3
    m = n - cut
    source = jnp.where(n < cut, (n >> 3) * 12 + (n & 7), (m >> 2) * 12 + 8 + (m & 3))
    perm = zero_one(col == source)
    out_a[...] = dot(perm, a_ref[...]).astype(BF16)
    out_b[...] = dot(perm, b_ref[...]).astype(BF16)


def sort_rows(a, b):
    rows, width = a.shape
    step = CHUNK * 3 // 2
    spec = pl.BlockSpec((step, width), lambda i: (i, 0))
    return pl.pallas_call(
        sort_kernel,
        grid=(rows // step,),
        in_specs=[spec, spec],
        out_specs=[spec, spec],
        out_shape=[jax.ShapeDtypeStruct((rows, width), BF16)] * 2,
        compiler_params=pltpu.CompilerParams(vmem_limit_bytes=VMEM_LIMIT),
        cost_estimate=pl.CostEstimate(
            flops=4 * rows * step * width, bytes_accessed=rows * width * 8, transcendentals=0
        ),
    )(a, b)


def fold_masks(out_rows, in_rows):
    n = lax.broadcasted_iota(jnp.int32, (out_rows, in_rows), 0)
    p = lax.broadcasted_iota(jnp.int32, (out_rows, in_rows), 1)
    low = (n >> 2) * 8 + (n & 3)
    return zero_one(p == low), zero_one(p == low + 4)


def unpack_into(packed_ref, rows_ref):
    packed = packed_ref.shape[0]
    width = rows_ref.shape[1]
    half = width // 2
    rows_ref[:packed, :] = packed_ref[:, :width]
    low, high = fold_masks(packed // 2, packed)
    rest = packed_ref[:, width:]
    rows_ref[packed:, :half] = dot(low, rest).astype(BF16)
    rows_ref[packed:, half:] = dot(high, rest).astype(BF16)


def unpack(packed):
    total, wide = packed.shape
    width = wide * 2 // 3
    return pl.pallas_call(
        unpack_into,
        grid=(total // CHUNK,),
        in_specs=[pl.BlockSpec((CHUNK, wide), lambda i: (i, 0))],
        out_specs=pl.BlockSpec((CHUNK * 3 // 2, width), lambda i: (i, 0)),
        out_shape=jax.ShapeDtypeStruct((total * 3 // 2, width), BF16),
        compiler_params=pltpu.CompilerParams(vmem_limit_bytes=VMEM_LIMIT),
        cost_estimate=pl.CostEstimate(
            flops=total * CHUNK * width * 2, bytes_accessed=total * wide * 4, transcendentals=0
        ),
    )(packed)


def expert_kernel(
    packed_ref,
    gate_ref,
    a_ref,
    b_ref,
    wg_ref,
    wu_ref,
    wd_ref,
    back_ref,
    rows_ref,
    hidden_ref,
    pregate_ref,
    preup_ref,
    slot_gate_ref,
):
    packed = packed_ref.shape[0]
    width = rows_ref.shape[1]
    half = width // 2
    unpack_into(packed_ref, rows_ref)
    back_hidden = lax.dot_general(rows_ref[...], wd_ref[...], NT, preferred_element_type=F32)
    a = a_ref[...].astype(F32)
    b = b_ref[...].astype(F32)
    scale = gate_ref[...]
    sig = jax.nn.sigmoid(a)
    swish = a * sig
    hidden = swish * b
    hidden_ref[...] = (hidden * scale).astype(BF16)
    slot_gate_ref[...] = jnp.sum(hidden * back_hidden, axis=1, keepdims=True)
    hidden_grad = scale * back_hidden
    pregate = (hidden_grad * b * sig * (1.0 + a * (1.0 - sig))).astype(BF16)
    preup = (hidden_grad * swish).astype(BF16)
    pregate_ref[...] = pregate
    preup_ref[...] = preup
    slot_grad = (
        lax.dot_general(pregate, wg_ref[...], NT, preferred_element_type=F32)
        + lax.dot_general(preup, wu_ref[...], NT, preferred_element_type=F32)
    ).astype(BF16)
    back_ref[:, :width] = slot_grad[:packed, :]
    p = lax.broadcasted_iota(jnp.int32, (packed, packed // 2), 0)
    n = lax.broadcasted_iota(jnp.int32, (packed, packed // 2), 1)
    same = n == (p >> 3) * 4 + (p & 3)
    first = (p & 7) < 4
    rest = slot_grad[packed:, :]
    back_ref[:, width:] = (
        dot(zero_one(same & first), rest[:, :half])
        + dot(zero_one(same & jnp.logical_not(first)), rest[:, half:])
    ).astype(BF16)


def expert(packed, gates, a, b, weight_gate, weight_up, weight_down):
    total, wide = packed.shape
    rows = total * 3 // 2
    hidden_units, width = weight_down.shape
    step = CHUNK * 3 // 2
    narrow = pl.BlockSpec((step, hidden_units), lambda i: (i, 0))
    column = pl.BlockSpec((step, 1), lambda i: (i, 0))
    packed_spec = pl.BlockSpec((CHUNK, wide), lambda i: (i, 0))
    return pl.pallas_call(
        expert_kernel,
        grid=(total // CHUNK,),
        in_specs=[
            packed_spec,
            column,
            narrow,
            narrow,
            pl.BlockSpec(weight_gate.shape, lambda i: (0, 0)),
            pl.BlockSpec(weight_up.shape, lambda i: (0, 0)),
            pl.BlockSpec(weight_down.shape, lambda i: (0, 0)),
        ],
        out_specs=[
            packed_spec,
            pl.BlockSpec((step, width), lambda i: (i, 0)),
            narrow,
            narrow,
            narrow,
            column,
        ],
        out_shape=[
            jax.ShapeDtypeStruct((total, wide), BF16),
            jax.ShapeDtypeStruct((rows, width), BF16),
            jax.ShapeDtypeStruct((rows, hidden_units), BF16),
            jax.ShapeDtypeStruct((rows, hidden_units), BF16),
            jax.ShapeDtypeStruct((rows, hidden_units), BF16),
            jax.ShapeDtypeStruct((rows, 1), F32),
        ],
        compiler_params=pltpu.CompilerParams(vmem_limit_bytes=VMEM_LIMIT),
        cost_estimate=pl.CostEstimate(
            flops=6 * rows * width * hidden_units,
            bytes_accessed=total * wide * 6,
            transcendentals=rows * hidden_units,
        ),
    )(packed, gates, a, b, weight_gate, weight_up, weight_down)


def combine_kernel(dest_ref, packed_ref, out_ref, acc_ref):
    step = pl.program_id(0)
    toks, width = out_ref.shape
    half = width // 2
    rows = packed_ref.shape[0]
    index = lax.broadcasted_iota(jnp.int32, (toks, rows), 1) + step * rows
    id_a, id_b, first = packed_ids(index)
    hit_a = dest_ref[:, 0:1] == id_a
    hit_b = dest_ref[:, 0:1] == id_b
    for k in range(1, dest_ref.shape[1]):
        d = dest_ref[:, k : k + 1]
        hit_a = hit_a | (d == id_a)
        hit_b = hit_b | (d == id_b)
    rest = packed_ref[:, width:]
    one_a = zero_one(hit_a)

    @pl.when(step == 0)
    def _():
        acc_ref[...] = jnp.zeros_like(acc_ref)

    acc_ref[:, :half] += dot(one_a, packed_ref[:, :half]) + dot(zero_one(hit_b & first), rest)
    acc_ref[:, half:] += dot(one_a, packed_ref[:, half:width]) + dot(
        zero_one(hit_b & jnp.logical_not(first)), rest
    )

    @pl.when(step == pl.num_programs(0) - 1)
    def _():
        out_ref[...] = acc_ref[...].astype(BF16)


def combine(dest, packed, toks):
    total, wide = packed.shape
    width = wide * 2 // 3
    return pl.pallas_call(
        combine_kernel,
        grid=(total // CHUNK,),
        in_specs=[
            pl.BlockSpec(dest.shape, lambda i: (0, 0)),
            pl.BlockSpec((CHUNK, wide), lambda i: (i, 0)),
        ],
        out_specs=pl.BlockSpec((toks, width), lambda i: (0, 0)),
        out_shape=jax.ShapeDtypeStruct((toks, width), BF16),
        scratch_shapes=[pltpu.VMEM((toks, width), F32)],
        compiler_params=pltpu.CompilerParams(vmem_limit_bytes=VMEM_LIMIT),
        cost_estimate=pl.CostEstimate(
            flops=2 * total * toks * width * 2, bytes_accessed=total * wide * 2, transcendentals=0
        ),
    )(dest, packed)


def exchange(x):
    return lax.all_to_all(x, AXES, split_axis=0, concat_axis=0, tiled=True)


def gather_all(x):
    return lax.all_gather(x, AXES, axis=0, tiled=False)


def sort_pairs(x, experts):
    x = x.reshape(experts * 8 // CHUNK, CHUNK // 8, 12)
    first = x[:, :, :8].reshape(x.shape[0], -1)
    last = x[:, :, 8:].reshape(x.shape[0], -1)
    return jnp.concatenate([first, last], axis=1).reshape(-1)


def unsort_pairs(x, experts):
    chunks = experts * 8 // CHUNK
    x = x.reshape(chunks, -1)
    first = x[:, :CHUNK].reshape(chunks, CHUNK // 8, 8)
    last = x[:, CHUNK:].reshape(chunks, CHUNK // 8, 4)
    return jnp.concatenate([first, last], axis=2).reshape(-1)


def body(
    tokens,
    grad_out,
    expert_ids,
    pair_slot,
    gate_weights,
    weight_gate,
    weight_up,
    weight_down,
    saved_gate,
    saved_up,
):
    experts = lax.axis_size("group") * lax.axis_size("member")
    me = lax.axis_index("group") * lax.axis_size("member") + lax.axis_index("member")
    toks, width = tokens.shape
    route_count = expert_ids.shape[1]
    pair_rows = saved_gate.shape[1] // experts
    packed_rows = experts * 8
    dest = expert_ids * pair_rows + pair_slot
    dest_t = expert_ids.T * pair_rows + pair_slot.T

    sent_grads = pack(dest_t, grad_out, packed_rows)
    here_grads = exchange(sent_grads)
    here_tokens = exchange(pack(dest_t, tokens, packed_rows))

    all_dest = gather_all(dest_t).reshape(experts, 1, -1)
    all_gates = gather_all(gate_weights.T).reshape(experts, 1, -1)
    wanted = (me * pair_rows + jnp.arange(pair_rows, dtype=jnp.int32))[None, :, None]
    gates = jnp.sum(jnp.where(all_dest == wanted, all_gates.astype(F32), 0.0), axis=2)
    gates = sort_pairs(gates, experts)[:, None]
    a, b = sort_rows(saved_gate[0], saved_up[0])

    back, grad_rows, hidden, pregate, preup, slot_gate = expert(
        here_grads, gates, a, b, weight_gate[0], weight_up[0], weight_down[0]
    )
    back_packed = exchange(back)

    slot_gate = unsort_pairs(slot_gate.astype(BF16)[:, 0], experts)
    all_slot_gates = gather_all(slot_gate)
    mine = lax.dynamic_slice(all_slot_gates, (0, me * pair_rows), (experts, pair_rows))
    grad_gates = jnp.take(mine.reshape(-1), dest.reshape(-1), axis=0, mode="clip")

    token_rows = unpack(here_tokens)
    over_rows = (((0,), (0,)), ((), ()))
    down_total = lax.dot_general(hidden, grad_rows, over_rows, preferred_element_type=F32)
    gate_total = lax.dot_general(token_rows, pregate, over_rows, preferred_element_type=F32)
    up_total = lax.dot_general(token_rows, preup, over_rows, preferred_element_type=F32)

    grad_tokens = combine(dest, back_packed, toks)
    return (
        grad_tokens,
        grad_gates.reshape(toks, route_count),
        gate_total[None].astype(BF16),
        up_total[None].astype(BF16),
        down_total[None].astype(BF16),
    )


def solution(mesh):
    rows = P(AXES, None)
    blocks = P(AXES, None, None)
    return jax.shard_map(
        body,
        mesh=mesh,
        in_specs=(rows,) * 5 + (blocks,) * 5,
        out_specs=(rows, rows, blocks, blocks, blocks),
        check_vma=False,
    )
```

```python
import jax
import jax.numpy as jnp
from jax import lax
from jax.experimental import pallas as pl
from jax.experimental.pallas import tpu as pltpu
from jax.sharding import PartitionSpec as P

F32 = jnp.float32
BF16 = jnp.bfloat16
AXES = ("group", "member")
CHUNK = 256
NT = (((1,), (1,)), ((), ()))
VMEM_LIMIT = 56 * 1024 * 1024

EXTRA = 128


def zero_one(mask):
    return jnp.where(mask, 1.0, 0.0).astype(BF16)


def dot(a, b):
    return jnp.dot(a, b, preferred_element_type=F32)


def packed_ids(index):
    pair, q = index >> 3, index & 7
    return pair * 12 + q, pair * 12 + 8 + (q & 3), q < 4


def side_by_side(a, b):
    lane = lax.broadcasted_iota(jnp.int32, (a.shape[0], EXTRA), 1)
    return jnp.where(lane < EXTRA // 2, a, b).astype(BF16)


def pack_kernel(dest_ref, gate_ref, x_ref, out_ref):
    rows, toks = out_ref.shape[0], x_ref.shape[0]
    width = x_ref.shape[1]
    half = width // 2
    index = lax.broadcasted_iota(jnp.int32, (rows, toks), 0) + pl.program_id(0) * rows
    id_a, id_b, first = packed_ids(index)
    hit_a = dest_ref[0:1, :] == id_a
    hit_b = dest_ref[0:1, :] == id_b
    for k in range(1, dest_ref.shape[0]):
        d = dest_ref[k : k + 1, :]
        hit_a = hit_a | (d == id_a)
        hit_b = hit_b | (d == id_b)
    out_ref[:, :width] = dot(zero_one(hit_a), x_ref[...]).astype(BF16)
    low = dot(zero_one(hit_b & first), x_ref[:, :half])
    high = dot(zero_one(hit_b & jnp.logical_not(first)), x_ref[:, half:])
    out_ref[:, width : width + half] = (low + high).astype(BF16)
    if out_ref.shape[1] > width + half:
        gate_a = jnp.zeros((rows, toks), F32)
        gate_b = jnp.zeros((rows, toks), F32)
        for k in range(dest_ref.shape[0]):
            d = dest_ref[k : k + 1, :]
            g = gate_ref[k : k + 1, :]
            gate_a = jnp.where(d == id_a, g, gate_a)
            gate_b = jnp.where(d == id_b, g, gate_b)
        out_ref[:, width + half :] = side_by_side(
            jnp.sum(gate_a, axis=1, keepdims=True), jnp.sum(gate_b, axis=1, keepdims=True)
        )


def pack(dest_t, gates_t, x, packed_rows, extra):
    toks, width = x.shape
    wide = width * 3 // 2 + extra
    return pl.pallas_call(
        pack_kernel,
        grid=(packed_rows // CHUNK,),
        in_specs=[
            pl.BlockSpec(dest_t.shape, lambda i: (0, 0)),
            pl.BlockSpec(gates_t.shape, lambda i: (0, 0)),
            pl.BlockSpec(x.shape, lambda i: (0, 0)),
        ],
        out_specs=pl.BlockSpec((CHUNK, wide), lambda i: (i, 0)),
        out_shape=jax.ShapeDtypeStruct((packed_rows, wide), BF16),
        compiler_params=pltpu.CompilerParams(vmem_limit_bytes=VMEM_LIMIT),
        cost_estimate=pl.CostEstimate(
            flops=2 * packed_rows * toks * width * 2,
            bytes_accessed=packed_rows * width * 3,
            transcendentals=0,
        ),
    )(dest_t, gates_t, x)


def sort_kernel(a_ref, b_ref, out_a, out_b):
    rows = a_ref.shape[0]
    n = lax.broadcasted_iota(jnp.int32, (rows, rows), 0)
    col = lax.broadcasted_iota(jnp.int32, (rows, rows), 1)
    cut = rows * 2 // 3
    m = n - cut
    source = jnp.where(n < cut, (n >> 3) * 12 + (n & 7), (m >> 2) * 12 + 8 + (m & 3))
    perm = zero_one(col == source)
    out_a[...] = dot(perm, a_ref[...]).astype(BF16)
    out_b[...] = dot(perm, b_ref[...]).astype(BF16)


def sort_rows(a, b):
    rows, width = a.shape
    step = CHUNK * 3 // 2
    spec = pl.BlockSpec((step, width), lambda i: (i, 0))
    return pl.pallas_call(
        sort_kernel,
        grid=(rows // step,),
        in_specs=[spec, spec],
        out_specs=[spec, spec],
        out_shape=[jax.ShapeDtypeStruct((rows, width), BF16)] * 2,
        compiler_params=pltpu.CompilerParams(vmem_limit_bytes=VMEM_LIMIT),
        cost_estimate=pl.CostEstimate(
            flops=4 * rows * step * width, bytes_accessed=rows * width * 8, transcendentals=0
        ),
    )(a, b)


def fold_masks(out_rows, in_rows):
    n = lax.broadcasted_iota(jnp.int32, (out_rows, in_rows), 0)
    p = lax.broadcasted_iota(jnp.int32, (out_rows, in_rows), 1)
    low = (n >> 2) * 8 + (n & 3)
    return zero_one(p == low), zero_one(p == low + 4)


def unpack_into(packed_ref, rows_ref):
    packed = packed_ref.shape[0]
    width = rows_ref.shape[1]
    half = width // 2
    rows_ref[:packed, :] = packed_ref[:, :width]
    low, high = fold_masks(packed // 2, packed)
    rest = packed_ref[:, width : width + half]
    rows_ref[packed:, :half] = dot(low, rest).astype(BF16)
    rows_ref[packed:, half:] = dot(high, rest).astype(BF16)


def unpack(packed):
    total, wide = packed.shape
    width = wide * 2 // 3
    return pl.pallas_call(
        unpack_into,
        grid=(total // CHUNK,),
        in_specs=[pl.BlockSpec((CHUNK, wide), lambda i: (i, 0))],
        out_specs=pl.BlockSpec((CHUNK * 3 // 2, width), lambda i: (i, 0)),
        out_shape=jax.ShapeDtypeStruct((total * 3 // 2, width), BF16),
        compiler_params=pltpu.CompilerParams(vmem_limit_bytes=VMEM_LIMIT),
        cost_estimate=pl.CostEstimate(
            flops=total * CHUNK * width * 2, bytes_accessed=total * wide * 4, transcendentals=0
        ),
    )(packed)


def expert_kernel(
    packed_ref,
    a_ref,
    b_ref,
    wg_ref,
    wu_ref,
    wd_ref,
    back_ref,
    rows_ref,
    hidden_ref,
    pregate_ref,
    preup_ref,
    scale_ref,
):
    packed = packed_ref.shape[0]
    width = rows_ref.shape[1]
    half = width // 2
    unpack_into(packed_ref, rows_ref)
    back_hidden = lax.dot_general(rows_ref[...], wd_ref[...], NT, preferred_element_type=F32)
    a = a_ref[...].astype(F32)
    b = b_ref[...].astype(F32)
    extra = packed_ref[:, width + half :]
    scale_ref[:packed, :] = extra[:, :1].astype(F32)
    scale_ref[packed:, :] = dot(fold_masks(packed // 2, packed)[0], extra)[:, EXTRA // 2 : EXTRA // 2 + 1]
    scale = scale_ref[...]
    sig = jax.nn.sigmoid(a)
    swish = a * sig
    hidden = swish * b
    hidden_ref[...] = (hidden * scale).astype(BF16)
    slot_gate = jnp.sum(hidden * back_hidden, axis=1, keepdims=True).astype(BF16)
    hidden_grad = scale * back_hidden
    pregate = (hidden_grad * b * sig * (1.0 + a * (1.0 - sig))).astype(BF16)
    preup = (hidden_grad * swish).astype(BF16)
    pregate_ref[...] = pregate
    preup_ref[...] = preup
    slot_grad = (
        lax.dot_general(pregate, wg_ref[...], NT, preferred_element_type=F32)
        + lax.dot_general(preup, wu_ref[...], NT, preferred_element_type=F32)
    ).astype(BF16)
    back_ref[:, :width] = slot_grad[:packed, :]
    p = lax.broadcasted_iota(jnp.int32, (packed, packed // 2), 0)
    n = lax.broadcasted_iota(jnp.int32, (packed, packed // 2), 1)
    same = n == (p >> 3) * 4 + (p & 3)
    first = (p & 7) < 4
    rest = slot_grad[packed:, :]
    back_ref[:, width : width + half] = (
        dot(zero_one(same & first), rest[:, :half])
        + dot(zero_one(same & jnp.logical_not(first)), rest[:, half:])
    ).astype(BF16)
    last = jnp.broadcast_to(slot_gate[packed:, :], (packed // 2, EXTRA))
    back_ref[:, width + half :] = side_by_side(
        slot_gate[:packed, :].astype(F32), dot(zero_one(same), last)
    )


def expert(packed, a, b, weight_gate, weight_up, weight_down):
    total, wide = packed.shape
    rows = a.shape[0]
    hidden_units, width = weight_down.shape
    step = CHUNK * 3 // 2
    narrow = pl.BlockSpec((step, hidden_units), lambda i: (i, 0))
    packed_spec = pl.BlockSpec((CHUNK, wide), lambda i: (i, 0))
    return pl.pallas_call(
        expert_kernel,
        grid=(total // CHUNK,),
        in_specs=[
            packed_spec,
            narrow,
            narrow,
            pl.BlockSpec(weight_gate.shape, lambda i: (0, 0)),
            pl.BlockSpec(weight_up.shape, lambda i: (0, 0)),
            pl.BlockSpec(weight_down.shape, lambda i: (0, 0)),
        ],
        out_specs=[
            packed_spec,
            pl.BlockSpec((step, width), lambda i: (i, 0)),
            narrow,
            narrow,
            narrow,
        ],
        out_shape=[
            jax.ShapeDtypeStruct((total, wide), BF16),
            jax.ShapeDtypeStruct((rows, width), BF16),
            jax.ShapeDtypeStruct((rows, hidden_units), BF16),
            jax.ShapeDtypeStruct((rows, hidden_units), BF16),
            jax.ShapeDtypeStruct((rows, hidden_units), BF16),
        ],
        scratch_shapes=[pltpu.VMEM((step, 1), F32)],
        compiler_params=pltpu.CompilerParams(vmem_limit_bytes=VMEM_LIMIT),
        cost_estimate=pl.CostEstimate(
            flops=6 * rows * width * hidden_units,
            bytes_accessed=total * wide * 6,
            transcendentals=rows * hidden_units,
        ),
    )(packed, a, b, weight_gate, weight_up, weight_down)


def combine_kernel(dest_ref, packed_ref, out_ref, gate_ref, acc_ref, gate_acc_ref):
    step = pl.program_id(0)
    toks, width = out_ref.shape
    half = width // 2
    rows = packed_ref.shape[0]
    index = lax.broadcasted_iota(jnp.int32, (toks, rows), 1) + step * rows
    id_a, id_b, first = packed_ids(index)

    @pl.when(step == 0)
    def _():
        acc_ref[...] = jnp.zeros_like(acc_ref)
        gate_acc_ref[...] = jnp.zeros_like(gate_acc_ref)

    extra = packed_ref[:, width + half :]
    lane = lax.broadcasted_iota(jnp.int32, (16, EXTRA), 1)
    pick = lax.broadcasted_iota(jnp.int32, (16, EXTRA), 0) * (EXTRA // 2)
    values = lax.dot_general(zero_one(lane == pick), extra, NT, preferred_element_type=F32)
    value_a = values[0:1, :]
    value_b = jnp.where(first[:1, :], values[1:2, :], 0.0)
    column = lax.broadcasted_iota(jnp.int32, gate_acc_ref.shape, 1)
    hit_a = index < 0
    hit_b = index < 0
    gates = gate_acc_ref[...]
    for k in range(dest_ref.shape[1]):
        d = dest_ref[:, k : k + 1]
        here_a = d == id_a
        here_b = d == id_b
        hit_a = hit_a | here_a
        hit_b = hit_b | here_b
        found = jnp.where(here_a, value_a, jnp.where(here_b, value_b, 0.0))
        gates += jnp.where(column == k, jnp.sum(found, axis=1, keepdims=True), 0.0)
    gate_acc_ref[...] = gates
    rest = packed_ref[:, width : width + half]
    one_a = zero_one(hit_a)

    acc_ref[:, :half] += dot(one_a, packed_ref[:, :half]) + dot(zero_one(hit_b & first), rest)
    acc_ref[:, half:] += dot(one_a, packed_ref[:, half:width]) + dot(
        zero_one(hit_b & jnp.logical_not(first)), rest
    )

    @pl.when(step == pl.num_programs(0) - 1)
    def _():
        out_ref[...] = acc_ref[...].astype(BF16)
        gate_ref[...] = gates[:, : gate_ref.shape[1]].astype(BF16)


def combine(dest, packed, width):
    toks, routes = dest.shape
    total, wide = packed.shape
    return pl.pallas_call(
        combine_kernel,
        grid=(total // CHUNK,),
        in_specs=[
            pl.BlockSpec(dest.shape, lambda i: (0, 0)),
            pl.BlockSpec((CHUNK, wide), lambda i: (i, 0)),
        ],
        out_specs=[
            pl.BlockSpec((toks, width), lambda i: (0, 0)),
            pl.BlockSpec((toks, routes), lambda i: (0, 0)),
        ],
        out_shape=[
            jax.ShapeDtypeStruct((toks, width), BF16),
            jax.ShapeDtypeStruct((toks, routes), BF16),
        ],
        scratch_shapes=[pltpu.VMEM((toks, width), F32), pltpu.VMEM((toks, EXTRA), F32)],
        compiler_params=pltpu.CompilerParams(vmem_limit_bytes=VMEM_LIMIT),
        cost_estimate=pl.CostEstimate(
            flops=2 * total * toks * width * 2, bytes_accessed=total * wide * 2, transcendentals=0
        ),
    )(dest, packed)


def exchange(x):
    return lax.all_to_all(x, AXES, split_axis=0, concat_axis=0, tiled=True)


def body(
    tokens,
    grad_out,
    expert_ids,
    pair_slot,
    gate_weights,
    weight_gate,
    weight_up,
    weight_down,
    saved_gate,
    saved_up,
):
    experts = lax.axis_size("group") * lax.axis_size("member")
    width = tokens.shape[1]
    pair_rows = saved_gate.shape[1] // experts
    packed_rows = experts * 8
    dest = expert_ids * pair_rows + pair_slot
    dest_t = expert_ids.T * pair_rows + pair_slot.T

    gates_t = gate_weights.T.astype(F32)
    here_grads = exchange(pack(dest_t, gates_t, grad_out, packed_rows, EXTRA))
    here_tokens = exchange(pack(dest_t, gates_t, tokens, packed_rows, 0))
    a, b = sort_rows(saved_gate[0], saved_up[0])
    back, grad_rows, hidden, pregate, preup = expert(
        here_grads, a, b, weight_gate[0], weight_up[0], weight_down[0]
    )
    back_packed = exchange(back)

    token_rows = unpack(here_tokens)
    over_rows = (((0,), (0,)), ((), ()))
    down_total = lax.dot_general(hidden, grad_rows, over_rows, preferred_element_type=F32)
    gate_total = lax.dot_general(token_rows, pregate, over_rows, preferred_element_type=F32)
    up_total = lax.dot_general(token_rows, preup, over_rows, preferred_element_type=F32)

    grad_tokens, grad_gates = combine(dest, back_packed, width)
    return (
        grad_tokens,
        grad_gates,
        gate_total[None].astype(BF16),
        up_total[None].astype(BF16),
        down_total[None].astype(BF16),
    )


def solution(mesh):
    rows = P(AXES, None)
    blocks = P(AXES, None, None)
    return jax.shard_map(
        body,
        mesh=mesh,
        in_specs=(rows,) * 5 + (blocks,) * 5,
        out_specs=(rows, rows, blocks, blocks, blocks),
        check_vma=False,
    )
```

```python
import jax
import jax.numpy as jnp
from jax import lax
from jax.experimental import pallas as pl
from jax.experimental.pallas import tpu as pltpu
from jax.sharding import PartitionSpec as P

F32 = jnp.float32
BF16 = jnp.bfloat16
AXES = ("group", "member")
CHUNK = 256
NT = (((1,), (1,)), ((), ()))
VMEM_LIMIT = 56 * 1024 * 1024

EXTRA = 128


def zero_one(mask):
    return jnp.where(mask, 1.0, 0.0).astype(BF16)


def dot(a, b):
    return jnp.dot(a, b, preferred_element_type=F32)


def packed_ids(index):
    pair, q = index >> 3, index & 7
    return pair * 12 + q, pair * 12 + 8 + (q & 3), q < 4


def side_by_side(a, b):
    lane = lax.broadcasted_iota(jnp.int32, (a.shape[0], EXTRA), 1)
    return jnp.where(lane < EXTRA // 2, a, b).astype(BF16)


def pack_kernel(ids_ref, slot_ref, gate_ref, x_ref, out_ref):
    dest = ids_ref[...] * 12 + slot_ref[...]
    rows, toks = out_ref.shape[0], x_ref.shape[0]
    width = x_ref.shape[1]
    half = width // 2
    index = lax.broadcasted_iota(jnp.int32, (rows, toks), 0) + pl.program_id(0) * rows
    id_a, id_b, first = packed_ids(index)
    gate = gate_ref[...].astype(F32)
    hit_a = index < 0
    hit_b = index < 0
    gate_a = jnp.zeros((rows, toks), F32)
    gate_b = jnp.zeros((rows, toks), F32)
    for k in range(dest.shape[0]):
        d, g = dest[k : k + 1, :], gate[k : k + 1, :]
        here_a = d == id_a
        here_b = d == id_b
        hit_a = hit_a | here_a
        hit_b = hit_b | here_b
        gate_a = jnp.where(here_a, g, gate_a)
        gate_b = jnp.where(here_b, g, gate_b)
    out_ref[:, :width] = dot(zero_one(hit_a), x_ref[...]).astype(BF16)
    low = dot(zero_one(hit_b & first), x_ref[:, :half])
    high = dot(zero_one(hit_b & jnp.logical_not(first)), x_ref[:, half:])
    out_ref[:, width : width + half] = (low + high).astype(BF16)
    out_ref[:, width + half :] = side_by_side(
        jnp.sum(gate_a, axis=1, keepdims=True), jnp.sum(gate_b, axis=1, keepdims=True)
    )


def pack(ids_t, slot_t, gates_t, x, packed_rows):
    toks, width = x.shape
    wide = width * 3 // 2 + EXTRA
    return pl.pallas_call(
        pack_kernel,
        grid=(packed_rows // CHUNK,),
        in_specs=[
            pl.BlockSpec(ids_t.shape, lambda i: (0, 0)),
            pl.BlockSpec(slot_t.shape, lambda i: (0, 0)),
            pl.BlockSpec(gates_t.shape, lambda i: (0, 0)),
            pl.BlockSpec(x.shape, lambda i: (0, 0)),
        ],
        out_specs=pl.BlockSpec((CHUNK, wide), lambda i: (i, 0)),
        out_shape=jax.ShapeDtypeStruct((packed_rows, wide), BF16),
        compiler_params=pltpu.CompilerParams(vmem_limit_bytes=VMEM_LIMIT),
        cost_estimate=pl.CostEstimate(
            flops=2 * packed_rows * toks * width * 2,
            bytes_accessed=packed_rows * width * 3,
            transcendentals=0,
        ),
    )(ids_t, slot_t, gates_t, x)


def sort_kernel(a_ref, b_ref, out_a, out_b):
    rows = a_ref.shape[0]
    n = lax.broadcasted_iota(jnp.int32, (rows, rows), 0)
    col = lax.broadcasted_iota(jnp.int32, (rows, rows), 1)
    cut = rows * 2 // 3
    m = n - cut
    source = jnp.where(n < cut, (n >> 3) * 12 + (n & 7), (m >> 2) * 12 + 8 + (m & 3))
    perm = zero_one(col == source)
    out_a[...] = dot(perm, a_ref[...]).astype(BF16)
    out_b[...] = dot(perm, b_ref[...]).astype(BF16)


def sort_rows(a, b):
    rows, width = a.shape
    step = CHUNK * 3 // 2
    spec = pl.BlockSpec((step, width), lambda i: (i, 0))
    return pl.pallas_call(
        sort_kernel,
        grid=(rows // step,),
        in_specs=[spec, spec],
        out_specs=[spec, spec],
        out_shape=[jax.ShapeDtypeStruct((rows, width), BF16)] * 2,
        compiler_params=pltpu.CompilerParams(vmem_limit_bytes=VMEM_LIMIT),
        cost_estimate=pl.CostEstimate(
            flops=4 * rows * step * width, bytes_accessed=rows * width * 8, transcendentals=0
        ),
    )(a, b)


def fold_masks(out_rows, in_rows):
    n = lax.broadcasted_iota(jnp.int32, (out_rows, in_rows), 0)
    p = lax.broadcasted_iota(jnp.int32, (out_rows, in_rows), 1)
    low = (n >> 2) * 8 + (n & 3)
    return zero_one(p == low), zero_one(p == low + 4)


def unpack_into(packed_ref, rows_ref):
    packed = packed_ref.shape[0]
    width = rows_ref.shape[1]
    half = width // 2
    rows_ref[:packed, :] = packed_ref[:, :width]
    low, high = fold_masks(packed // 2, packed)
    rest = packed_ref[:, width : width + half]
    rows_ref[packed:, :half] = dot(low, rest).astype(BF16)
    rows_ref[packed:, half:] = dot(high, rest).astype(BF16)


def spread_kernel(x_ref, out_ref):
    groups, rows, width = out_ref.shape
    toks = x_ref.shape[0]
    me = lax.axis_index("member")
    extra = x_ref[:, width:]
    lane = lax.broadcasted_iota(jnp.int32, (16, EXTRA), 1)
    pick = zero_one(lane == lax.broadcasted_iota(jnp.int32, (16, EXTRA), 0))
    table = lax.dot_general(pick, extra, NT, preferred_element_type=F32).astype(jnp.int32)
    ids, slots = table[:8, :], table[8:, :]
    source = lax.broadcasted_iota(jnp.int32, (8, toks), 1) >> 7
    keys = jnp.where((ids & 7) == me, (ids >> 3) * 12 + slots + source * 256, -1)
    index = lax.broadcasted_iota(jnp.int32, (groups * rows, 1), 0)
    group = (index * 1366) >> 16
    row = index - group * rows
    early = row < rows * 2 // 3
    late = row - rows * 2 // 3
    wanted = group * 12 + jnp.where(
        early, (row & 7) + (row >> 3) * 256, 8 + (late & 3) + (late >> 2) * 256
    )
    hit = keys[0:1, :] == wanted
    for k in range(1, 8):
        hit = hit | (keys[k : k + 1, :] == wanted)
    moved = dot(zero_one(hit), x_ref[:, :width]).astype(BF16)
    out_ref[...] = moved.reshape(out_ref.shape)


def spread(x, groups, width):
    total, wide = x.shape
    step = total // 2
    return pl.pallas_call(
        spread_kernel,
        grid=(2,),
        in_specs=[pl.BlockSpec((step, wide), lambda i: (i, 0))],
        out_specs=pl.BlockSpec((groups, 48, width), lambda i: (0, i, 0)),
        out_shape=jax.ShapeDtypeStruct((groups, 96, width), BF16),
        compiler_params=pltpu.CompilerParams(vmem_limit_bytes=VMEM_LIMIT),
        cost_estimate=pl.CostEstimate(
            flops=2 * groups * 96 * step * width,
            bytes_accessed=2 * (total * wide + groups * 96 * width),
            transcendentals=0,
        ),
    )(x)


def collect_kernel(x_ref, out_ref):
    late = out_ref.shape[0] * 2 // 3
    for group in range(x_ref.shape[0]):
        for part in range(2):
            at = part * 48
            to = (group * 2 + part) * 32
            out_ref[to : to + 32, :] = x_ref[group, at : at + 32, :]
            to = late + (group * 2 + part) * 16
            out_ref[to : to + 16, :] = x_ref[group, at + 32 : at + 48, :]


def collect(x):
    groups, rows, width = x.shape
    return pl.pallas_call(
        collect_kernel,
        grid=(groups // 4,),
        in_specs=[pl.BlockSpec((4, rows, width), lambda i: (i, 0, 0))],
        out_specs=pl.BlockSpec((4 * rows, width), lambda i: (i, 0)),
        out_shape=jax.ShapeDtypeStruct((groups * rows, width), BF16),
        compiler_params=pltpu.CompilerParams(vmem_limit_bytes=VMEM_LIMIT),
        cost_estimate=pl.CostEstimate(
            flops=0, bytes_accessed=groups * rows * width * 4, transcendentals=0
        ),
    )(x)


def expert_kernel(
    packed_ref,
    a_ref,
    b_ref,
    wg_ref,
    wu_ref,
    wd_ref,
    back_ref,
    rows_ref,
    hidden_ref,
    pregate_ref,
    preup_ref,
    scale_ref,
):
    packed = packed_ref.shape[0]
    width = rows_ref.shape[1]
    half = width // 2
    unpack_into(packed_ref, rows_ref)
    back_hidden = lax.dot_general(rows_ref[...], wd_ref[...], NT, preferred_element_type=F32)
    a = a_ref[...].astype(F32)
    b = b_ref[...].astype(F32)
    extra = packed_ref[:, width + half :]
    scale_ref[:packed, :] = extra[:, :1].astype(F32)
    scale_ref[packed:, :] = dot(fold_masks(packed // 2, packed)[0], extra)[:, EXTRA // 2 : EXTRA // 2 + 1]
    scale = scale_ref[...]
    sig = jax.nn.sigmoid(a)
    swish = a * sig
    hidden = swish * b
    hidden_ref[...] = (hidden * scale).astype(BF16)
    slot_gate = jnp.sum(hidden * back_hidden, axis=1, keepdims=True).astype(BF16)
    hidden_grad = scale * back_hidden
    pregate = (hidden_grad * b * sig * (1.0 + a * (1.0 - sig))).astype(BF16)
    preup = (hidden_grad * swish).astype(BF16)
    pregate_ref[...] = pregate
    preup_ref[...] = preup
    slot_grad = (
        lax.dot_general(pregate, wg_ref[...], NT, preferred_element_type=F32)
        + lax.dot_general(preup, wu_ref[...], NT, preferred_element_type=F32)
    ).astype(BF16)
    back_ref[:, :width] = slot_grad[:packed, :]
    p = lax.broadcasted_iota(jnp.int32, (packed, packed // 2), 0)
    n = lax.broadcasted_iota(jnp.int32, (packed, packed // 2), 1)
    same = n == (p >> 3) * 4 + (p & 3)
    first = (p & 7) < 4
    rest = slot_grad[packed:, :]
    back_ref[:, width : width + half] = (
        dot(zero_one(same & first), rest[:, :half])
        + dot(zero_one(same & jnp.logical_not(first)), rest[:, half:])
    ).astype(BF16)
    last = jnp.broadcast_to(slot_gate[packed:, :], (packed // 2, EXTRA))
    back_ref[:, width + half :] = side_by_side(
        slot_gate[:packed, :].astype(F32), dot(zero_one(same), last)
    )


def expert(packed, a, b, weight_gate, weight_up, weight_down):
    total, wide = packed.shape
    rows = a.shape[0]
    hidden_units, width = weight_down.shape
    step = CHUNK * 3 // 2
    narrow = pl.BlockSpec((step, hidden_units), lambda i: (i, 0))
    packed_spec = pl.BlockSpec((CHUNK, wide), lambda i: (i, 0))
    return pl.pallas_call(
        expert_kernel,
        grid=(total // CHUNK,),
        in_specs=[
            packed_spec,
            narrow,
            narrow,
            pl.BlockSpec(weight_gate.shape, lambda i: (0, 0)),
            pl.BlockSpec(weight_up.shape, lambda i: (0, 0)),
            pl.BlockSpec(weight_down.shape, lambda i: (0, 0)),
        ],
        out_specs=[
            packed_spec,
            pl.BlockSpec((step, width), lambda i: (i, 0)),
            narrow,
            narrow,
            narrow,
        ],
        out_shape=[
            jax.ShapeDtypeStruct((total, wide), BF16),
            jax.ShapeDtypeStruct((rows, width), BF16),
            jax.ShapeDtypeStruct((rows, hidden_units), BF16),
            jax.ShapeDtypeStruct((rows, hidden_units), BF16),
            jax.ShapeDtypeStruct((rows, hidden_units), BF16),
        ],
        scratch_shapes=[pltpu.VMEM((step, 1), F32)],
        compiler_params=pltpu.CompilerParams(vmem_limit_bytes=VMEM_LIMIT),
        cost_estimate=pl.CostEstimate(
            flops=6 * rows * width * hidden_units,
            bytes_accessed=total * wide * 6,
            transcendentals=rows * hidden_units,
        ),
    )(packed, a, b, weight_gate, weight_up, weight_down)


def combine_kernel(dest_ref, packed_ref, out_ref, gate_ref, acc_ref, gate_acc_ref):
    step = pl.program_id(0)
    toks, width = out_ref.shape
    half = width // 2
    rows = packed_ref.shape[0]
    index = lax.broadcasted_iota(jnp.int32, (toks, rows), 1) + step * rows
    id_a, id_b, first = packed_ids(index)

    @pl.when(step == 0)
    def _():
        acc_ref[...] = jnp.zeros_like(acc_ref)
        gate_acc_ref[...] = jnp.zeros_like(gate_acc_ref)

    extra = packed_ref[:, width + half :]
    lane = lax.broadcasted_iota(jnp.int32, (16, EXTRA), 1)
    pick = lax.broadcasted_iota(jnp.int32, (16, EXTRA), 0) * (EXTRA // 2)
    values = lax.dot_general(zero_one(lane == pick), extra, NT, preferred_element_type=F32)
    value_a = values[0:1, :]
    value_b = jnp.where(first[:1, :], values[1:2, :], 0.0)
    column = lax.broadcasted_iota(jnp.int32, gate_acc_ref.shape, 1)
    hit_a = index < 0
    hit_b = index < 0
    gates = gate_acc_ref[...]
    for k in range(dest_ref.shape[1]):
        d = dest_ref[:, k : k + 1]
        here_a = d == id_a
        here_b = d == id_b
        hit_a = hit_a | here_a
        hit_b = hit_b | here_b
        found = jnp.where(here_a, value_a, jnp.where(here_b, value_b, 0.0))
        gates += jnp.where(column == k, jnp.sum(found, axis=1, keepdims=True), 0.0)
    gate_acc_ref[...] = gates
    rest = packed_ref[:, width : width + half]
    one_a = zero_one(hit_a)

    acc_ref[:, :half] += dot(one_a, packed_ref[:, :half]) + dot(zero_one(hit_b & first), rest)
    acc_ref[:, half:] += dot(one_a, packed_ref[:, half:width]) + dot(
        zero_one(hit_b & jnp.logical_not(first)), rest
    )

    @pl.when(step == pl.num_programs(0) - 1)
    def _():
        out_ref[...] = acc_ref[...].astype(BF16)
        row = lax.broadcasted_iota(jnp.int32, (16, EXTRA), 0)
        turned = lax.dot_general(
            zero_one(lane == row), gates.astype(BF16), NT, preferred_element_type=F32
        )
        gate_ref[...] = turned[: gate_ref.shape[0], :].astype(BF16)


def combine(dest, packed, width):
    toks, routes = dest.shape
    total, wide = packed.shape
    return pl.pallas_call(
        combine_kernel,
        grid=(total // CHUNK,),
        in_specs=[
            pl.BlockSpec(dest.shape, lambda i: (0, 0)),
            pl.BlockSpec((CHUNK, wide), lambda i: (i, 0)),
        ],
        out_specs=[
            pl.BlockSpec((toks, width), lambda i: (0, 0)),
            pl.BlockSpec((routes, toks), lambda i: (0, 0)),
        ],
        out_shape=[
            jax.ShapeDtypeStruct((toks, width), BF16),
            jax.ShapeDtypeStruct((routes, toks), BF16),
        ],
        scratch_shapes=[pltpu.VMEM((toks, width), F32), pltpu.VMEM((toks, EXTRA), F32)],
        compiler_params=pltpu.CompilerParams(vmem_limit_bytes=VMEM_LIMIT),
        cost_estimate=pl.CostEstimate(
            flops=2 * total * toks * width * 2, bytes_accessed=total * wide * 2, transcendentals=0
        ),
    )(dest, packed)


def exchange(x, axes):
    return lax.all_to_all(x, axes, split_axis=0, concat_axis=0, tiled=True)


def body(
    tokens,
    grad_out,
    expert_ids,
    pair_slot,
    gate_weights,
    weight_gate,
    weight_up,
    weight_down,
    saved_gate,
    saved_up,
):
    experts = lax.axis_size("group") * lax.axis_size("member")
    width = tokens.shape[1]
    pair_rows = saved_gate.shape[1] // experts
    packed_rows = experts * 8
    dest = expert_ids * pair_rows + pair_slot
    sent_grads = pack(expert_ids.T, pair_slot.T, gate_weights.T, grad_out, packed_rows)
    sent_grads, expert_ids, tokens = lax.optimization_barrier((sent_grads, expert_ids, tokens))
    routes = jnp.concatenate([expert_ids, pair_slot], axis=1).astype(BF16)
    routes = jnp.pad(routes, ((0, 0), (0, EXTRA - routes.shape[1])))
    line_tokens = lax.all_gather(
        jnp.concatenate([tokens, routes], axis=1), "member", axis=0, tiled=True
    )
    here_grads = exchange(sent_grads, AXES)
    sent_tokens = spread(line_tokens, lax.axis_size("group"), width)
    here_grads, sent_tokens = lax.optimization_barrier((here_grads, sent_tokens))
    here_tokens = exchange(sent_tokens, "group")
    a, b = sort_rows(saved_gate[0], saved_up[0])
    back, grad_rows, hidden, pregate, preup = expert(
        here_grads, a, b, weight_gate[0], weight_up[0], weight_down[0]
    )
    back, here_tokens = lax.optimization_barrier((back, here_tokens))
    back_packed = exchange(back, AXES)

    token_rows = collect(here_tokens)
    over_rows = (((0,), (0,)), ((), ()))
    down_total = lax.dot_general(hidden, grad_rows, over_rows, preferred_element_type=F32)
    gate_total = lax.dot_general(token_rows, pregate, over_rows, preferred_element_type=F32)
    up_total = lax.dot_general(token_rows, preup, over_rows, preferred_element_type=F32)

    grad_tokens, grad_gates = combine(dest, back_packed, width)
    return (
        grad_tokens,
        grad_gates.T,
        gate_total[None].astype(BF16),
        up_total[None].astype(BF16),
        down_total[None].astype(BF16),
    )


def solution(mesh):
    rows = P(AXES, None)
    blocks = P(AXES, None, None)
    return jax.shard_map(
        body,
        mesh=mesh,
        in_specs=(rows,) * 5 + (blocks,) * 5,
        out_specs=(rows, rows, blocks, blocks, blocks),
        check_vma=False,
    )
```

```python
import functools

import jax
import jax.numpy as jnp
from jax import lax
from jax.experimental import pallas as pl
from jax.experimental.pallas import tpu as pltpu
from jax.sharding import PartitionSpec as P

F32 = jnp.float32
BF16 = jnp.bfloat16
AXES = ("group", "member")
CHUNK = 256
NT = (((1,), (1,)), ((), ()))
VMEM_LIMIT = 56 * 1024 * 1024

EXTRA = 128


def zero_one(mask):
    return jnp.where(mask, 1.0, 0.0).astype(BF16)


def dot(a, b):
    return jnp.dot(a, b, preferred_element_type=F32)


def packed_ids(index):
    pair, q = index >> 3, index & 7
    return pair * 12 + q, pair * 12 + 8 + (q & 3), q < 4


def side_by_side(a, b):
    lane = lax.broadcasted_iota(jnp.int32, (a.shape[0], EXTRA), 1)
    return jnp.where(lane < EXTRA // 2, a, b).astype(BF16)


def pack_kernel(scaled, ids_ref, slot_ref, gate_ref, x_ref, out_ref, halves_ref):
    rows, toks = out_ref.shape[0], x_ref.shape[0]
    width = x_ref.shape[1]
    half = width // 2

    @pl.when(pl.program_id(0) == 0)
    def _():
        halves_ref[:toks, :] = x_ref[:, :half]
        halves_ref[toks:, :] = x_ref[:, half:]

    index = lax.broadcasted_iota(jnp.int32, (rows, toks), 0) + pl.program_id(0) * rows
    id_a, id_b, first = packed_ids(index)
    dest = ids_ref[...] * 12 + slot_ref[...]
    gate = gate_ref[...].astype(F32) if scaled else jnp.ones(dest.shape, F32)
    weight_a = jnp.zeros((rows, toks), F32)
    weight_b = jnp.zeros((rows, toks), F32)
    for k in range(dest.shape[0]):
        d, g = dest[k : k + 1, :], gate[k : k + 1, :]
        weight_a = jnp.where(d == id_a, g, weight_a)
        weight_b = jnp.where(d == id_b, g, weight_b)
    out_ref[:, :width] = dot(weight_a.astype(BF16), x_ref[...]).astype(BF16)
    low = jnp.where(first, weight_b, 0.0).astype(BF16)
    high = jnp.where(first, 0.0, weight_b).astype(BF16)
    out_ref[:, width:] = dot(
        jnp.concatenate([low, high], axis=1), halves_ref[...]
    ).astype(BF16)


def pack(ids_t, slot_t, gates_t, x, packed_rows, scaled):
    toks, width = x.shape
    wide = width * 3 // 2
    return pl.pallas_call(
        functools.partial(pack_kernel, scaled),
        grid=(packed_rows // CHUNK,),
        in_specs=[
            pl.BlockSpec(ids_t.shape, lambda i: (0, 0)),
            pl.BlockSpec(slot_t.shape, lambda i: (0, 0)),
            pl.BlockSpec(gates_t.shape, lambda i: (0, 0)),
            pl.BlockSpec(x.shape, lambda i: (0, 0)),
        ],
        out_specs=pl.BlockSpec((CHUNK, wide), lambda i: (i, 0)),
        out_shape=jax.ShapeDtypeStruct((packed_rows, wide), BF16),
        scratch_shapes=[pltpu.VMEM((2 * toks, width // 2), BF16)],
        compiler_params=pltpu.CompilerParams(vmem_limit_bytes=VMEM_LIMIT),
        cost_estimate=pl.CostEstimate(
            flops=2 * packed_rows * toks * width * 2,
            bytes_accessed=packed_rows * width * 3,
            transcendentals=0,
        ),
    )(ids_t, slot_t, gates_t, x)


def sort_kernel(a_ref, b_ref, out_a, out_b):
    rows = a_ref.shape[0]
    n = lax.broadcasted_iota(jnp.int32, (rows, rows), 0)
    col = lax.broadcasted_iota(jnp.int32, (rows, rows), 1)
    cut = rows * 2 // 3
    m = n - cut
    source = jnp.where(n < cut, (n >> 3) * 12 + (n & 7), (m >> 2) * 12 + 8 + (m & 3))
    perm = zero_one(col == source)
    out_a[...] = dot(perm, a_ref[...]).astype(BF16)
    out_b[...] = dot(perm, b_ref[...]).astype(BF16)


def sort_rows(a, b):
    rows, width = a.shape
    step = CHUNK * 3 // 2
    spec = pl.BlockSpec((step, width), lambda i: (i, 0))
    return pl.pallas_call(
        sort_kernel,
        grid=(rows // step,),
        in_specs=[spec, spec],
        out_specs=[spec, spec],
        out_shape=[jax.ShapeDtypeStruct((rows, width), BF16)] * 2,
        compiler_params=pltpu.CompilerParams(vmem_limit_bytes=VMEM_LIMIT),
        cost_estimate=pl.CostEstimate(
            flops=4 * rows * step * width, bytes_accessed=rows * width * 8, transcendentals=0
        ),
    )(a, b)


def fold_masks(out_rows, in_rows):
    n = lax.broadcasted_iota(jnp.int32, (out_rows, in_rows), 0)
    p = lax.broadcasted_iota(jnp.int32, (out_rows, in_rows), 1)
    low = (n >> 2) * 8 + (n & 3)
    return zero_one(p == low), zero_one(p == low + 4)


def unpack_into(packed_ref, rows_ref):
    packed = packed_ref.shape[0]
    width = rows_ref.shape[1]
    half = width // 2
    rows_ref[:packed, :] = packed_ref[:, :width]
    low, high = fold_masks(packed // 2, packed)
    rest = packed_ref[:, width : width + half]
    rows_ref[packed:, :half] = dot(low, rest).astype(BF16)
    rows_ref[packed:, half:] = dot(high, rest).astype(BF16)


def unpack(packed):
    total, wide = packed.shape
    width = wide * 2 // 3
    return pl.pallas_call(
        unpack_into,
        grid=(total // CHUNK,),
        in_specs=[pl.BlockSpec((CHUNK, wide), lambda i: (i, 0))],
        out_specs=pl.BlockSpec((CHUNK * 3 // 2, width), lambda i: (i, 0)),
        out_shape=jax.ShapeDtypeStruct((total * 3 // 2, width), BF16),
        compiler_params=pltpu.CompilerParams(vmem_limit_bytes=VMEM_LIMIT),
        cost_estimate=pl.CostEstimate(
            flops=total * CHUNK * width * 2, bytes_accessed=total * wide * 4, transcendentals=0
        ),
    )(packed)


def expert_kernel(
    packed_ref,
    a_ref,
    b_ref,
    wg_ref,
    wu_ref,
    wd_ref,
    back_ref,
    rows_ref,
    hidden_ref,
    pregate_ref,
    preup_ref,
):
    packed = packed_ref.shape[0]
    width = rows_ref.shape[1]
    half = width // 2
    unpack_into(packed_ref, rows_ref)
    back_hidden = lax.dot_general(rows_ref[...], wd_ref[...], NT, preferred_element_type=F32)
    a = a_ref[...].astype(F32)
    b = b_ref[...].astype(F32)
    sig = jax.nn.sigmoid(a)
    swish = a * sig
    hidden = swish * b
    hidden_ref[...] = hidden.astype(BF16)
    slot_gate = jnp.sum(hidden * back_hidden, axis=1, keepdims=True).astype(BF16)
    pregate = (back_hidden * b * sig * (1.0 + a * (1.0 - sig))).astype(BF16)
    preup = (back_hidden * swish).astype(BF16)
    pregate_ref[...] = pregate
    preup_ref[...] = preup
    slot_grad = (
        lax.dot_general(pregate, wg_ref[...], NT, preferred_element_type=F32)
        + lax.dot_general(preup, wu_ref[...], NT, preferred_element_type=F32)
    ).astype(BF16)
    back_ref[:, :width] = slot_grad[:packed, :]
    p = lax.broadcasted_iota(jnp.int32, (packed, packed // 2), 0)
    n = lax.broadcasted_iota(jnp.int32, (packed, packed // 2), 1)
    same = n == (p >> 3) * 4 + (p & 3)
    first = (p & 7) < 4
    rest = slot_grad[packed:, :]
    back_ref[:, width : width + half] = (
        dot(zero_one(same & first), rest[:, :half])
        + dot(zero_one(same & jnp.logical_not(first)), rest[:, half:])
    ).astype(BF16)
    last = jnp.broadcast_to(slot_gate[packed:, :], (packed // 2, EXTRA))
    back_ref[:, width + half :] = side_by_side(
        slot_gate[:packed, :].astype(F32), dot(zero_one(same), last)
    )


def expert(packed, a, b, weight_gate, weight_up, weight_down):
    total, wide = packed.shape
    rows = a.shape[0]
    hidden_units, width = weight_down.shape
    step = CHUNK * 3 // 2
    narrow = pl.BlockSpec((step, hidden_units), lambda i: (i, 0))
    packed_spec = pl.BlockSpec((CHUNK, wide), lambda i: (i, 0))
    back_spec = pl.BlockSpec((CHUNK, wide + EXTRA), lambda i: (i, 0))
    return pl.pallas_call(
        expert_kernel,
        grid=(total // CHUNK,),
        in_specs=[
            packed_spec,
            narrow,
            narrow,
            pl.BlockSpec(weight_gate.shape, lambda i: (0, 0)),
            pl.BlockSpec(weight_up.shape, lambda i: (0, 0)),
            pl.BlockSpec(weight_down.shape, lambda i: (0, 0)),
        ],
        out_specs=[
            back_spec,
            pl.BlockSpec((step, width), lambda i: (i, 0)),
            narrow,
            narrow,
            narrow,
        ],
        out_shape=[
            jax.ShapeDtypeStruct((total, wide + EXTRA), BF16),
            jax.ShapeDtypeStruct((rows, width), BF16),
            jax.ShapeDtypeStruct((rows, hidden_units), BF16),
            jax.ShapeDtypeStruct((rows, hidden_units), BF16),
            jax.ShapeDtypeStruct((rows, hidden_units), BF16),
        ],
        compiler_params=pltpu.CompilerParams(vmem_limit_bytes=VMEM_LIMIT),
        cost_estimate=pl.CostEstimate(
            flops=6 * rows * width * hidden_units,
            bytes_accessed=total * wide * 6,
            transcendentals=rows * hidden_units,
        ),
    )(packed, a, b, weight_gate, weight_up, weight_down)


def combine_kernel(ids_ref, slot_ref, gate_ref, packed_ref, out_ref, terms_ref, acc_ref, term_acc_ref):
    step = pl.program_id(0)
    toks, width = out_ref.shape
    half = width // 2
    rows = packed_ref.shape[0]
    index = lax.broadcasted_iota(jnp.int32, (toks, rows), 1) + step * rows
    id_a, id_b, first = packed_ids(index)

    @pl.when(step == 0)
    def _():
        acc_ref[...] = jnp.zeros_like(acc_ref)
        term_acc_ref[...] = jnp.zeros_like(term_acc_ref)

    hit_a = index < 0
    hit_b = index < 0
    for k in range(ids_ref.shape[1]):
        d = ids_ref[:, k : k + 1] * 12 + slot_ref[:, k : k + 1]
        hit_a = hit_a | (d == id_a)
        hit_b = hit_b | (d == id_b)
    one_a = zero_one(hit_a)
    low = zero_one(hit_b & first)
    high = zero_one(hit_b & jnp.logical_not(first))
    rest = packed_ref[:, width : width + half]
    acc_ref[:, :half] += dot(one_a, packed_ref[:, :half]) + dot(low, rest)
    acc_ref[:, half:] += dot(one_a, packed_ref[:, half:width]) + dot(high, rest)

    extra = packed_ref[:, width + half :]
    lane = lax.broadcasted_iota(jnp.int32, (rows, EXTRA), 1)
    pair = (lax.broadcasted_iota(jnp.int32, (rows, EXTRA), 0) + step * rows) >> 3
    zero = jnp.zeros((), BF16)
    value_a = jnp.where(lane == pair, extra[:, :1], zero)
    value_b = jnp.where(lane == pair, extra[:, EXTRA // 2 : EXTRA // 2 + 1], zero)
    term_acc_ref[...] += dot(one_a, value_a) + dot(low, value_b)

    @pl.when(step == pl.num_programs(0) - 1)
    def _():
        out_ref[...] = acc_ref[...].astype(BF16)
        terms = term_acc_ref[...]
        expert_lane = lax.broadcasted_iota(jnp.int32, terms.shape, 1)
        found = jnp.zeros(terms.shape, F32)
        for k in range(ids_ref.shape[1]):
            mine = jnp.where(expert_lane == ids_ref[:, k : k + 1], terms, 0.0)
            term = jnp.sum(mine, axis=1, keepdims=True) / gate_ref[:, k : k + 1].astype(F32)
            found = jnp.where(expert_lane == k, term, found)
        row = lax.broadcasted_iota(jnp.int32, (16, EXTRA), 0)
        column = lax.broadcasted_iota(jnp.int32, (16, EXTRA), 1)
        turned = lax.dot_general(
            zero_one(column == row), found.astype(BF16), NT, preferred_element_type=F32
        )
        terms_ref[...] = turned[: terms_ref.shape[0], :].astype(BF16)


def combine(ids, slots, gates, packed, width):
    toks, routes = ids.shape
    total, wide = packed.shape
    table = pl.BlockSpec(ids.shape, lambda i: (0, 0))
    return pl.pallas_call(
        combine_kernel,
        grid=(total // CHUNK,),
        in_specs=[table, table, table, pl.BlockSpec((CHUNK, wide), lambda i: (i, 0))],
        out_specs=[
            pl.BlockSpec((toks, width), lambda i: (0, 0)),
            pl.BlockSpec((routes, toks), lambda i: (0, 0)),
        ],
        out_shape=[
            jax.ShapeDtypeStruct((toks, width), BF16),
            jax.ShapeDtypeStruct((routes, toks), BF16),
        ],
        scratch_shapes=[pltpu.VMEM((toks, width), F32), pltpu.VMEM((toks, EXTRA), F32)],
        compiler_params=pltpu.CompilerParams(vmem_limit_bytes=VMEM_LIMIT),
        cost_estimate=pl.CostEstimate(
            flops=2 * total * toks * width * 2, bytes_accessed=total * wide * 2, transcendentals=0
        ),
    )(ids, slots, gates, packed)


def exchange(x, axes):
    return lax.all_to_all(x, axes, split_axis=0, concat_axis=0, tiled=True)


def body(
    tokens,
    grad_out,
    expert_ids,
    pair_slot,
    gate_weights,
    weight_gate,
    weight_up,
    weight_down,
    saved_gate,
    saved_up,
):
    experts = lax.axis_size("group") * lax.axis_size("member")
    width = tokens.shape[1]
    packed_rows = experts * 8
    routing = (expert_ids.T, pair_slot.T, gate_weights.T)

    here_grads = exchange(pack(*routing, grad_out, packed_rows, True), AXES)
    here_tokens = exchange(pack(*routing, tokens, packed_rows, False), AXES)
    a, b = sort_rows(saved_gate[0], saved_up[0])
    back, grad_rows, hidden, pregate, preup = expert(
        here_grads, a, b, weight_gate[0], weight_up[0], weight_down[0]
    )
    back, here_tokens = lax.optimization_barrier((back, here_tokens))
    back_packed = exchange(back, AXES)

    token_rows = unpack(here_tokens)
    over_rows = (((0,), (0,)), ((), ()))
    down_total = lax.dot_general(hidden, grad_rows, over_rows, preferred_element_type=F32)
    gate_total = lax.dot_general(token_rows, pregate, over_rows, preferred_element_type=F32)
    up_total = lax.dot_general(token_rows, preup, over_rows, preferred_element_type=F32)

    grad_tokens, grad_gates = combine(expert_ids, pair_slot, gate_weights, back_packed, width)
    return (
        grad_tokens,
        grad_gates.T,
        gate_total[None].astype(BF16),
        up_total[None].astype(BF16),
        down_total[None].astype(BF16),
    )


def solution(mesh):
    rows = P(AXES, None)
    blocks = P(AXES, None, None)
    return jax.shard_map(
        body,
        mesh=mesh,
        in_specs=(rows,) * 5 + (blocks,) * 5,
        out_specs=(rows, rows, blocks, blocks, blocks),
        check_vma=False,
    )
```

```python
import functools

import jax
import jax.numpy as jnp
from jax import lax
from jax.experimental import pallas as pl
from jax.experimental.pallas import tpu as pltpu
from jax.sharding import PartitionSpec as P

F32 = jnp.float32
BF16 = jnp.bfloat16
AXES = ("group", "member")
CHUNK = 256
BLOCK = 128
LOAD = 256
NT = (((1,), (1,)), ((), ()))
VMEM_LIMIT = 56 * 1024 * 1024

EXTRA = 128


def zero_one(mask):
    return jnp.where(mask, 1.0, 0.0).astype(BF16)


def dot(a, b):
    return jnp.dot(a, b, preferred_element_type=F32)


def packed_ids(index):
    pair, q = index >> 3, index & 7
    return pair * 12 + q, pair * 12 + 8 + (q & 3), q < 4


def side_by_side(a, b):
    lane = lax.broadcasted_iota(jnp.int32, (a.shape[0], EXTRA), 1)
    return jnp.where(lane < EXTRA // 2, a, b).astype(BF16)


def pack_kernel(scaled, ids_ref, slot_ref, gate_ref, x_ref, out_ref, halves_ref, made_ref, sems):
    toks, width = x_ref.shape
    half = width // 2
    rows = BLOCK
    halves_ref[:toks, :] = x_ref[:, :half]
    halves_ref[toks:, :] = x_ref[:, half:]
    dest = ids_ref[...] * 12 + slot_ref[...]
    gate = gate_ref[...].astype(F32) if scaled else jnp.ones(dest.shape, F32)
    copies = []
    for block in range(made_ref.shape[0] // rows):
        index = lax.broadcasted_iota(jnp.int32, (rows, 1), 0) + block * rows
        id_a, id_b, first = packed_ids(index)
        id_low = jnp.where(first, id_b, -1)
        id_high = jnp.where(first, -1, id_b)
        weight_a = jnp.zeros((rows, toks), F32)
        low = jnp.zeros((rows, toks), F32)
        high = jnp.zeros((rows, toks), F32)
        for k in range(dest.shape[0]):
            d, g = dest[k : k + 1, :], gate[k : k + 1, :]
            weight_a = jnp.where(d == id_a, g, weight_a)
            low = jnp.where(d == id_low, g, low)
            high = jnp.where(d == id_high, g, high)
        here = pl.ds(block * rows, rows)
        made_ref[here, :width] = dot(weight_a.astype(BF16), x_ref[...]).astype(BF16)
        made_ref[here, width:] = dot(
            jnp.concatenate([low, high], axis=1).astype(BF16), halves_ref[...]
        ).astype(BF16)
        copy = pltpu.make_async_copy(made_ref.at[here, :], out_ref.at[here, :], sems.at[block])
        copy.start()
        copies.append(copy)
    for copy in copies:
        copy.wait()


def pack(ids_t, slot_t, gates_t, x, packed_rows, scaled):
    toks, width = x.shape
    wide = width * 3 // 2
    return pl.pallas_call(
        functools.partial(pack_kernel, scaled),
        out_specs=pl.BlockSpec(memory_space=pl.ANY),
        out_shape=jax.ShapeDtypeStruct((packed_rows, wide), BF16),
        scratch_shapes=[
            pltpu.VMEM((2 * toks, width // 2), BF16),
            pltpu.VMEM((packed_rows, wide), BF16),
            pltpu.SemaphoreType.DMA((packed_rows // BLOCK,)),
        ],
        compiler_params=pltpu.CompilerParams(vmem_limit_bytes=VMEM_LIMIT),
        cost_estimate=pl.CostEstimate(
            flops=2 * packed_rows * toks * width * 2,
            bytes_accessed=packed_rows * width * 3,
            transcendentals=0,
        ),
    )(ids_t, slot_t, gates_t, x)


def sort_kernel(a_ref, b_ref, out_a, out_b):
    rows = a_ref.shape[0]
    n = lax.broadcasted_iota(jnp.int32, (rows, rows), 0)
    col = lax.broadcasted_iota(jnp.int32, (rows, rows), 1)
    cut = rows * 2 // 3
    m = n - cut
    source = jnp.where(n < cut, (n >> 3) * 12 + (n & 7), (m >> 2) * 12 + 8 + (m & 3))
    perm = zero_one(col == source)
    out_a[...] = dot(perm, a_ref[...]).astype(BF16)
    out_b[...] = dot(perm, b_ref[...]).astype(BF16)


def sort_rows(a, b):
    rows, width = a.shape
    step = CHUNK * 3 // 2
    spec = pl.BlockSpec((step, width), lambda i: (i, 0))
    return pl.pallas_call(
        sort_kernel,
        grid=(rows // step,),
        in_specs=[spec, spec],
        out_specs=[spec, spec],
        out_shape=[jax.ShapeDtypeStruct((rows, width), BF16)] * 2,
        compiler_params=pltpu.CompilerParams(vmem_limit_bytes=VMEM_LIMIT),
        cost_estimate=pl.CostEstimate(
            flops=4 * rows * step * width, bytes_accessed=rows * width * 8, transcendentals=0
        ),
    )(a, b)


def fold_masks(out_rows, in_rows):
    n = lax.broadcasted_iota(jnp.int32, (out_rows, in_rows), 0)
    p = lax.broadcasted_iota(jnp.int32, (out_rows, in_rows), 1)
    low = (n >> 2) * 8 + (n & 3)
    return zero_one(p == low), zero_one(p == low + 4)


def unpack_into(packed_ref, rows_ref):
    packed = packed_ref.shape[0]
    width = rows_ref.shape[1]
    half = width // 2
    rows_ref[:packed, :] = packed_ref[:, :width]
    low, high = fold_masks(packed // 2, packed)
    rest = packed_ref[:, width : width + half]
    rows_ref[packed:, :half] = dot(low, rest).astype(BF16)
    rows_ref[packed:, half:] = dot(high, rest).astype(BF16)


def unpack(packed):
    total, wide = packed.shape
    width = wide * 2 // 3
    return pl.pallas_call(
        unpack_into,
        grid=(total // CHUNK,),
        in_specs=[pl.BlockSpec((CHUNK, wide), lambda i: (i, 0))],
        out_specs=pl.BlockSpec((CHUNK * 3 // 2, width), lambda i: (i, 0)),
        out_shape=jax.ShapeDtypeStruct((total * 3 // 2, width), BF16),
        compiler_params=pltpu.CompilerParams(vmem_limit_bytes=VMEM_LIMIT),
        cost_estimate=pl.CostEstimate(
            flops=total * CHUNK * width * 2, bytes_accessed=total * wide * 4, transcendentals=0
        ),
    )(packed)


def expert_kernel(
    packed_ref,
    a_ref,
    b_ref,
    wg_ref,
    wu_ref,
    wd_ref,
    back_ref,
    rows_ref,
    hidden_ref,
    pregate_ref,
    preup_ref,
):
    packed = packed_ref.shape[0]
    width = rows_ref.shape[1]
    half = width // 2
    unpack_into(packed_ref, rows_ref)
    back_hidden = lax.dot_general(rows_ref[...], wd_ref[...], NT, preferred_element_type=F32)
    a = a_ref[...].astype(F32)
    b = b_ref[...].astype(F32)
    sig = jax.nn.sigmoid(a)
    swish = a * sig
    hidden = swish * b
    hidden_ref[...] = hidden.astype(BF16)
    slot_gate = jnp.sum(hidden * back_hidden, axis=1, keepdims=True).astype(BF16)
    pregate = (back_hidden * b * sig * (1.0 + a * (1.0 - sig))).astype(BF16)
    preup = (back_hidden * swish).astype(BF16)
    pregate_ref[...] = pregate
    preup_ref[...] = preup
    slot_grad = (
        lax.dot_general(pregate, wg_ref[...], NT, preferred_element_type=F32)
        + lax.dot_general(preup, wu_ref[...], NT, preferred_element_type=F32)
    ).astype(BF16)
    back_ref[:, :width] = slot_grad[:packed, :]
    p = lax.broadcasted_iota(jnp.int32, (packed, packed // 2), 0)
    n = lax.broadcasted_iota(jnp.int32, (packed, packed // 2), 1)
    same = n == (p >> 3) * 4 + (p & 3)
    first = (p & 7) < 4
    rest = slot_grad[packed:, :]
    back_ref[:, width : width + half] = (
        dot(zero_one(same & first), rest[:, :half])
        + dot(zero_one(same & jnp.logical_not(first)), rest[:, half:])
    ).astype(BF16)
    last = jnp.broadcast_to(slot_gate[packed:, :], (packed // 2, EXTRA))
    back_ref[:, width + half :] = side_by_side(
        slot_gate[:packed, :].astype(F32), dot(zero_one(same), last)
    )


def expert(packed, a, b, weight_gate, weight_up, weight_down):
    total, wide = packed.shape
    rows = a.shape[0]
    hidden_units, width = weight_down.shape
    step = CHUNK * 3 // 2
    narrow = pl.BlockSpec((step, hidden_units), lambda i: (i, 0))
    packed_spec = pl.BlockSpec((CHUNK, wide), lambda i: (i, 0))
    back_spec = pl.BlockSpec((CHUNK, wide + EXTRA), lambda i: (i, 0))
    return pl.pallas_call(
        expert_kernel,
        grid=(total // CHUNK,),
        in_specs=[
            packed_spec,
            narrow,
            narrow,
            pl.BlockSpec(weight_gate.shape, lambda i: (0, 0)),
            pl.BlockSpec(weight_up.shape, lambda i: (0, 0)),
            pl.BlockSpec(weight_down.shape, lambda i: (0, 0)),
        ],
        out_specs=[
            back_spec,
            pl.BlockSpec((step, width), lambda i: (i, 0)),
            narrow,
            narrow,
            narrow,
        ],
        out_shape=[
            jax.ShapeDtypeStruct((total, wide + EXTRA), BF16),
            jax.ShapeDtypeStruct((rows, width), BF16),
            jax.ShapeDtypeStruct((rows, hidden_units), BF16),
            jax.ShapeDtypeStruct((rows, hidden_units), BF16),
            jax.ShapeDtypeStruct((rows, hidden_units), BF16),
        ],
        compiler_params=pltpu.CompilerParams(vmem_limit_bytes=VMEM_LIMIT),
        cost_estimate=pl.CostEstimate(
            flops=6 * rows * width * hidden_units,
            bytes_accessed=total * wide * 6,
            transcendentals=rows * hidden_units,
        ),
    )(packed, a, b, weight_gate, weight_up, weight_down)


def combine_kernel(
    ids_ref, slot_ref, gate_ref, packed_ref, out_ref, terms_ref, here_ref, masks_ref, sems
):
    toks, width = out_ref.shape
    half = width // 2
    total = here_ref.shape[0]
    rows = LOAD
    copies = []
    for block in range(total // rows):
        at = pl.ds(block * rows, rows)
        copy = pltpu.make_async_copy(packed_ref.at[at, :], here_ref.at[at, :], sems.at[block])
        copy.start()
        copies.append(copy)

    ids = ids_ref[...]
    dest = ids * 12 + slot_ref[...]
    columns = [jnp.broadcast_to(dest[:, k : k + 1], (toks, 128)) for k in range(dest.shape[1])]
    for start in range(0, total, 128):
        index = lax.broadcasted_iota(jnp.int32, (1, 128), 1) + start
        id_a, id_b, first = packed_ids(index)
        id_low = jnp.where(first, id_b, -1)
        id_high = jnp.where(first, -1, id_b)
        hits = [column == id_a for column in columns]
        lows = [column == id_low for column in columns]
        highs = [column == id_high for column in columns]
        for n, found in enumerate((hits, lows, highs)):
            mask = functools.reduce(jnp.logical_or, found)
            masks_ref[n * toks : (n + 1) * toks, start : start + 128] = zero_one(mask)

    terms = jnp.zeros((toks, EXTRA), F32)
    left = jnp.zeros((toks, half), F32)
    right = jnp.zeros((toks, half), F32)
    for block, copy in enumerate(copies):
        copy.wait()
        at = slice(block * rows, (block + 1) * rows)
        one_a = masks_ref[:toks, at]
        folded = dot(masks_ref[toks:, at], here_ref[at, width : width + half])
        left += dot(one_a, here_ref[at, :half]) + folded[:toks, :]
        right += dot(one_a, here_ref[at, half:width]) + folded[toks:, :]
        extra = here_ref[at, width + half :]
        lane = lax.broadcasted_iota(jnp.int32, (rows, EXTRA), 1)
        pair = (lax.broadcasted_iota(jnp.int32, (rows, EXTRA), 0) + block * rows) >> 3
        zero = jnp.zeros((), BF16)
        value_a = jnp.where(lane == pair, extra[:, :1], zero)
        value_b = jnp.where(lane == pair, extra[:, EXTRA // 2 : EXTRA // 2 + 1], zero)
        terms += dot(one_a, value_a) + dot(masks_ref[toks : 2 * toks, at], value_b)
    out_ref[:, :half] = left.astype(BF16)
    out_ref[:, half:] = right.astype(BF16)

    expert_lane = lax.broadcasted_iota(jnp.int32, terms.shape, 1)
    found = jnp.zeros(terms.shape, F32)
    for k in range(ids.shape[1]):
        mine = jnp.where(expert_lane == ids[:, k : k + 1], terms, 0.0)
        term = jnp.sum(mine, axis=1, keepdims=True) / gate_ref[:, k : k + 1].astype(F32)
        found = jnp.where(expert_lane == k, term, found)
    row = lax.broadcasted_iota(jnp.int32, (16, EXTRA), 0)
    column = lax.broadcasted_iota(jnp.int32, (16, EXTRA), 1)
    turned = lax.dot_general(
        zero_one(column == row), found.astype(BF16), NT, preferred_element_type=F32
    )
    terms_ref[...] = turned[: terms_ref.shape[0], :].astype(BF16)


def combine(ids, slots, gates, packed, width):
    toks, routes = ids.shape
    total, wide = packed.shape
    table = pl.BlockSpec(memory_space=pltpu.VMEM)
    return pl.pallas_call(
        combine_kernel,
        in_specs=[table, table, table, pl.BlockSpec(memory_space=pl.ANY)],
        out_shape=[
            jax.ShapeDtypeStruct((toks, width), BF16),
            jax.ShapeDtypeStruct((routes, toks), BF16),
        ],
        scratch_shapes=[
            pltpu.VMEM((total, wide), BF16),
            pltpu.VMEM((3 * toks, total), BF16),
            pltpu.SemaphoreType.DMA((total // LOAD,)),
        ],
        compiler_params=pltpu.CompilerParams(vmem_limit_bytes=VMEM_LIMIT),
        cost_estimate=pl.CostEstimate(
            flops=2 * total * toks * width * 2, bytes_accessed=total * wide * 2, transcendentals=0
        ),
    )(ids, slots, gates, packed)


def exchange(x, axes):
    return lax.all_to_all(x, axes, split_axis=0, concat_axis=0, tiled=True)


def body(
    tokens,
    grad_out,
    expert_ids,
    pair_slot,
    gate_weights,
    weight_gate,
    weight_up,
    weight_down,
    saved_gate,
    saved_up,
):
    experts = lax.axis_size("group") * lax.axis_size("member")
    width = tokens.shape[1]
    packed_rows = experts * 8
    routing = (expert_ids.T, pair_slot.T, gate_weights.T)

    here_grads = exchange(pack(*routing, grad_out, packed_rows, True), AXES)
    here_tokens = exchange(pack(*routing, tokens, packed_rows, False), AXES)
    a, b = sort_rows(saved_gate[0], saved_up[0])
    back, grad_rows, hidden, pregate, preup = expert(
        here_grads, a, b, weight_gate[0], weight_up[0], weight_down[0]
    )
    back, here_tokens = lax.optimization_barrier((back, here_tokens))
    back_packed = exchange(back, AXES)

    token_rows = unpack(here_tokens)
    over_rows = (((0,), (0,)), ((), ()))
    down_total = lax.dot_general(hidden, grad_rows, over_rows, preferred_element_type=F32)
    gate_total = lax.dot_general(token_rows, pregate, over_rows, preferred_element_type=F32)
    up_total = lax.dot_general(token_rows, preup, over_rows, preferred_element_type=F32)

    grad_tokens, grad_gates = combine(expert_ids, pair_slot, gate_weights, back_packed, width)
    return (
        grad_tokens,
        grad_gates.T,
        gate_total[None].astype(BF16),
        up_total[None].astype(BF16),
        down_total[None].astype(BF16),
    )


def solution(mesh):
    rows = P(AXES, None)
    blocks = P(AXES, None, None)
    return jax.shard_map(
        body,
        mesh=mesh,
        in_specs=(rows,) * 5 + (blocks,) * 5,
        out_specs=(rows, rows, blocks, blocks, blocks),
        check_vma=False,
    )
```

```python
import functools

import jax
import jax.numpy as jnp
from jax import lax
from jax.experimental import pallas as pl
from jax.experimental.pallas import tpu as pltpu
from jax.sharding import PartitionSpec as P

F32 = jnp.float32
BF16 = jnp.bfloat16
AXES = ("group", "member")
CHUNK = 256
BLOCK = 128
LOAD = 256
NT = (((1,), (1,)), ((), ()))
VMEM_LIMIT = 56 * 1024 * 1024
SMALL_VMEM = 20 * 1024 * 1024

EXTRA = 128


def zero_one(mask):
    return jnp.where(mask, 1.0, 0.0).astype(BF16)


def dot(a, b):
    return jnp.dot(a, b, preferred_element_type=F32)


def packed_ids(index):
    pair, q = index >> 3, index & 7
    return pair * 12 + q, pair * 12 + 8 + (q & 3), q < 4


def side_by_side(a, b):
    lane = lax.broadcasted_iota(jnp.int32, (a.shape[0], EXTRA), 1)
    return jnp.where(lane < EXTRA // 2, a, b).astype(BF16)


def pack_kernel(scaled, ids_ref, slot_ref, gate_ref, x_ref, out_ref, halves_ref, made_ref, sems):
    toks, width = x_ref.shape
    half = width // 2
    rows = BLOCK
    halves_ref[:toks, :] = x_ref[:, :half]
    halves_ref[toks:, :] = x_ref[:, half:]
    dest = ids_ref[...] * 12 + slot_ref[...]
    gate = gate_ref[...].astype(F32) if scaled else jnp.ones(dest.shape, F32)
    copies = []
    for block in range(made_ref.shape[0] // rows):
        index = lax.broadcasted_iota(jnp.int32, (rows, 1), 0) + block * rows
        id_a, id_b, first = packed_ids(index)
        id_low = jnp.where(first, id_b, -1)
        id_high = jnp.where(first, -1, id_b)
        weight_a = jnp.zeros((rows, toks), F32)
        low = jnp.zeros((rows, toks), F32)
        high = jnp.zeros((rows, toks), F32)
        for k in range(dest.shape[0]):
            d, g = dest[k : k + 1, :], gate[k : k + 1, :]
            weight_a = jnp.where(d == id_a, g, weight_a)
            low = jnp.where(d == id_low, g, low)
            high = jnp.where(d == id_high, g, high)
        here = pl.ds(block * rows, rows)
        made_ref[here, :width] = dot(weight_a.astype(BF16), x_ref[...]).astype(BF16)
        made_ref[here, width:] = dot(
            jnp.concatenate([low, high], axis=1).astype(BF16), halves_ref[...]
        ).astype(BF16)
        copy = pltpu.make_async_copy(made_ref.at[here, :], out_ref.at[here, :], sems.at[block])
        copy.start()
        copies.append(copy)
    for copy in copies:
        copy.wait()


def pack(ids_t, slot_t, gates_t, x, packed_rows, scaled):
    toks, width = x.shape
    wide = width * 3 // 2
    return pl.pallas_call(
        functools.partial(pack_kernel, scaled),
        out_specs=pl.BlockSpec(memory_space=pl.ANY),
        out_shape=jax.ShapeDtypeStruct((packed_rows, wide), BF16),
        scratch_shapes=[
            pltpu.VMEM((2 * toks, width // 2), BF16),
            pltpu.VMEM((packed_rows, wide), BF16),
            pltpu.SemaphoreType.DMA((packed_rows // BLOCK,)),
        ],
        compiler_params=pltpu.CompilerParams(vmem_limit_bytes=VMEM_LIMIT),
        cost_estimate=pl.CostEstimate(
            flops=2 * packed_rows * toks * width * 2,
            bytes_accessed=packed_rows * width * 3,
            transcendentals=0,
        ),
    )(ids_t, slot_t, gates_t, x)


def sort_kernel(a_ref, b_ref, out_a, out_b):
    rows = a_ref.shape[0]
    n = lax.broadcasted_iota(jnp.int32, (rows, rows), 0)
    col = lax.broadcasted_iota(jnp.int32, (rows, rows), 1)
    cut = rows * 2 // 3
    m = n - cut
    source = jnp.where(n < cut, (n >> 3) * 12 + (n & 7), (m >> 2) * 12 + 8 + (m & 3))
    perm = zero_one(col == source)
    out_a[...] = dot(perm, a_ref[...]).astype(BF16)
    out_b[...] = dot(perm, b_ref[...]).astype(BF16)


def sort_rows(a, b):
    rows, width = a.shape
    step = CHUNK * 3 // 2
    spec = pl.BlockSpec((step, width), lambda i: (i, 0))
    return pl.pallas_call(
        sort_kernel,
        grid=(rows // step,),
        in_specs=[spec, spec],
        out_specs=[spec, spec],
        out_shape=[jax.ShapeDtypeStruct((rows, width), BF16)] * 2,
        compiler_params=pltpu.CompilerParams(vmem_limit_bytes=VMEM_LIMIT),
        cost_estimate=pl.CostEstimate(
            flops=4 * rows * step * width, bytes_accessed=rows * width * 8, transcendentals=0
        ),
    )(a, b)


def fold_masks(out_rows, in_rows):
    n = lax.broadcasted_iota(jnp.int32, (out_rows, in_rows), 0)
    p = lax.broadcasted_iota(jnp.int32, (out_rows, in_rows), 1)
    low = (n >> 2) * 8 + (n & 3)
    return zero_one(p == low), zero_one(p == low + 4)


def unpack_into(packed_ref, rows_ref):
    packed = packed_ref.shape[0]
    width = rows_ref.shape[1]
    half = width // 2
    rows_ref[:packed, :] = packed_ref[:, :width]
    low, high = fold_masks(packed // 2, packed)
    rest = packed_ref[:, width : width + half]
    rows_ref[packed:, :half] = dot(low, rest).astype(BF16)
    rows_ref[packed:, half:] = dot(high, rest).astype(BF16)


def unpack(packed):
    total, wide = packed.shape
    width = wide * 2 // 3
    return pl.pallas_call(
        unpack_into,
        grid=(total // CHUNK,),
        in_specs=[pl.BlockSpec((CHUNK, wide), lambda i: (i, 0))],
        out_specs=pl.BlockSpec((CHUNK * 3 // 2, width), lambda i: (i, 0)),
        out_shape=jax.ShapeDtypeStruct((total * 3 // 2, width), BF16),
        compiler_params=pltpu.CompilerParams(vmem_limit_bytes=SMALL_VMEM),
        cost_estimate=pl.CostEstimate(
            flops=total * CHUNK * width * 2, bytes_accessed=total * wide * 4, transcendentals=0
        ),
    )(packed)


def expert_kernel(
    packed_ref,
    a_ref,
    b_ref,
    wg_ref,
    wu_ref,
    wd_ref,
    back_ref,
    rows_ref,
    hidden_ref,
    pregate_ref,
    preup_ref,
):
    packed = packed_ref.shape[0]
    width = rows_ref.shape[1]
    half = width // 2
    unpack_into(packed_ref, rows_ref)
    back_hidden = lax.dot_general(rows_ref[...], wd_ref[...], NT, preferred_element_type=F32)
    a = a_ref[...].astype(F32)
    b = b_ref[...].astype(F32)
    sig = jax.nn.sigmoid(a)
    swish = a * sig
    hidden = swish * b
    hidden_ref[...] = hidden.astype(BF16)
    slot_gate = jnp.sum(hidden * back_hidden, axis=1, keepdims=True).astype(BF16)
    pregate = (back_hidden * b * sig * (1.0 + a * (1.0 - sig))).astype(BF16)
    preup = (back_hidden * swish).astype(BF16)
    pregate_ref[...] = pregate
    preup_ref[...] = preup
    slot_grad = (
        lax.dot_general(pregate, wg_ref[...], NT, preferred_element_type=F32)
        + lax.dot_general(preup, wu_ref[...], NT, preferred_element_type=F32)
    ).astype(BF16)
    back_ref[:, :width] = slot_grad[:packed, :]
    p = lax.broadcasted_iota(jnp.int32, (packed, packed // 2), 0)
    n = lax.broadcasted_iota(jnp.int32, (packed, packed // 2), 1)
    same = n == (p >> 3) * 4 + (p & 3)
    first = (p & 7) < 4
    rest = slot_grad[packed:, :]
    back_ref[:, width : width + half] = (
        dot(zero_one(same & first), rest[:, :half])
        + dot(zero_one(same & jnp.logical_not(first)), rest[:, half:])
    ).astype(BF16)
    last = jnp.broadcast_to(slot_gate[packed:, :], (packed // 2, EXTRA))
    back_ref[:, width + half :] = side_by_side(
        slot_gate[:packed, :].astype(F32), dot(zero_one(same), last)
    )


def expert(packed, a, b, weight_gate, weight_up, weight_down):
    total, wide = packed.shape
    rows = a.shape[0]
    hidden_units, width = weight_down.shape
    step = CHUNK * 3 // 2
    narrow = pl.BlockSpec((step, hidden_units), lambda i: (i, 0))
    packed_spec = pl.BlockSpec((CHUNK, wide), lambda i: (i, 0))
    back_spec = pl.BlockSpec((CHUNK, wide + EXTRA), lambda i: (i, 0))
    return pl.pallas_call(
        expert_kernel,
        grid=(total // CHUNK,),
        in_specs=[
            packed_spec,
            narrow,
            narrow,
            pl.BlockSpec(weight_gate.shape, lambda i: (0, 0)),
            pl.BlockSpec(weight_up.shape, lambda i: (0, 0)),
            pl.BlockSpec(weight_down.shape, lambda i: (0, 0)),
        ],
        out_specs=[
            back_spec,
            pl.BlockSpec((step, width), lambda i: (i, 0)),
            narrow,
            narrow,
            narrow,
        ],
        out_shape=[
            jax.ShapeDtypeStruct((total, wide + EXTRA), BF16),
            jax.ShapeDtypeStruct((rows, width), BF16),
            jax.ShapeDtypeStruct((rows, hidden_units), BF16),
            jax.ShapeDtypeStruct((rows, hidden_units), BF16),
            jax.ShapeDtypeStruct((rows, hidden_units), BF16),
        ],
        compiler_params=pltpu.CompilerParams(vmem_limit_bytes=VMEM_LIMIT),
        cost_estimate=pl.CostEstimate(
            flops=6 * rows * width * hidden_units,
            bytes_accessed=total * wide * 6,
            transcendentals=rows * hidden_units,
        ),
    )(packed, a, b, weight_gate, weight_up, weight_down)


def combine_kernel(
    ids_ref, slot_ref, gate_ref, packed_ref, out_ref, terms_ref, here_ref, masks_ref, sems
):
    toks, width = out_ref.shape
    half = width // 2
    total = here_ref.shape[0]
    rows = LOAD
    copies = []
    for block in range(total // rows):
        at = pl.ds(block * rows, rows)
        copy = pltpu.make_async_copy(packed_ref.at[at, :], here_ref.at[at, :], sems.at[block])
        copy.start()
        copies.append(copy)

    ids = ids_ref[...]
    dest = ids * 12 + slot_ref[...]
    columns = [jnp.broadcast_to(dest[:, k : k + 1], (toks, 128)) for k in range(dest.shape[1])]
    for start in range(0, total, 128):
        index = lax.broadcasted_iota(jnp.int32, (1, 128), 1) + start
        id_a, id_b, first = packed_ids(index)
        id_low = jnp.where(first, id_b, -1)
        id_high = jnp.where(first, -1, id_b)
        hits = [column == id_a for column in columns]
        lows = [column == id_low for column in columns]
        highs = [column == id_high for column in columns]
        for n, found in enumerate((hits, lows, highs)):
            mask = functools.reduce(jnp.logical_or, found)
            masks_ref[n * toks : (n + 1) * toks, start : start + 128] = zero_one(mask)

    terms = jnp.zeros((toks, EXTRA), F32)
    left = jnp.zeros((toks, half), F32)
    right = jnp.zeros((toks, half), F32)
    for block, copy in enumerate(copies):
        copy.wait()
        at = slice(block * rows, (block + 1) * rows)
        one_a = masks_ref[:toks, at]
        folded = dot(masks_ref[toks:, at], here_ref[at, width : width + half])
        left += dot(one_a, here_ref[at, :half]) + folded[:toks, :]
        right += dot(one_a, here_ref[at, half:width]) + folded[toks:, :]
        extra = here_ref[at, width + half :]
        lane = lax.broadcasted_iota(jnp.int32, (rows, EXTRA), 1)
        pair = (lax.broadcasted_iota(jnp.int32, (rows, EXTRA), 0) + block * rows) >> 3
        zero = jnp.zeros((), BF16)
        value_a = jnp.where(lane == pair, extra[:, :1], zero)
        value_b = jnp.where(lane == pair, extra[:, EXTRA // 2 : EXTRA // 2 + 1], zero)
        terms += dot(one_a, value_a) + dot(masks_ref[toks : 2 * toks, at], value_b)
    out_ref[:, :half] = left.astype(BF16)
    out_ref[:, half:] = right.astype(BF16)

    expert_lane = lax.broadcasted_iota(jnp.int32, terms.shape, 1)
    found = jnp.zeros(terms.shape, F32)
    for k in range(ids.shape[1]):
        mine = jnp.where(expert_lane == ids[:, k : k + 1], terms, 0.0)
        term = jnp.sum(mine, axis=1, keepdims=True) / gate_ref[:, k : k + 1].astype(F32)
        found = jnp.where(expert_lane == k, term, found)
    row = lax.broadcasted_iota(jnp.int32, (16, EXTRA), 0)
    column = lax.broadcasted_iota(jnp.int32, (16, EXTRA), 1)
    turned = lax.dot_general(
        zero_one(column == row), found.astype(BF16), NT, preferred_element_type=F32
    )
    terms_ref[...] = turned[: terms_ref.shape[0], :].astype(BF16)


def combine(ids, slots, gates, packed, width):
    toks, routes = ids.shape
    total, wide = packed.shape
    table = pl.BlockSpec(memory_space=pltpu.VMEM)
    return pl.pallas_call(
        combine_kernel,
        in_specs=[table, table, table, pl.BlockSpec(memory_space=pl.ANY)],
        out_shape=[
            jax.ShapeDtypeStruct((toks, width), BF16),
            jax.ShapeDtypeStruct((routes, toks), BF16),
        ],
        scratch_shapes=[
            pltpu.VMEM((total, wide), BF16),
            pltpu.VMEM((3 * toks, total), BF16),
            pltpu.SemaphoreType.DMA((total // LOAD,)),
        ],
        compiler_params=pltpu.CompilerParams(vmem_limit_bytes=SMALL_VMEM),
        cost_estimate=pl.CostEstimate(
            flops=2 * total * toks * width * 2, bytes_accessed=total * wide * 2, transcendentals=0
        ),
    )(ids, slots, gates, packed)


def exchange(x, axes):
    return lax.all_to_all(x, axes, split_axis=0, concat_axis=0, tiled=True)


def body(
    tokens,
    grad_out,
    expert_ids,
    pair_slot,
    gate_weights,
    weight_gate,
    weight_up,
    weight_down,
    saved_gate,
    saved_up,
):
    experts = lax.axis_size("group") * lax.axis_size("member")
    width = tokens.shape[1]
    packed_rows = experts * 8
    routing = (expert_ids.T, pair_slot.T, gate_weights.T)

    here_grads = exchange(pack(*routing, grad_out, packed_rows, True), AXES)
    here_tokens = exchange(pack(*routing, tokens, packed_rows, False), AXES)
    a, b = sort_rows(saved_gate[0], saved_up[0])
    back, grad_rows, hidden, pregate, preup = expert(
        here_grads, a, b, weight_gate[0], weight_up[0], weight_down[0]
    )
    back, here_tokens = lax.optimization_barrier((back, here_tokens))
    back_packed = exchange(back, AXES)

    token_rows = unpack(here_tokens)
    over_rows = (((0,), (0,)), ((), ()))
    down_total = lax.dot_general(hidden, grad_rows, over_rows, preferred_element_type=F32)
    gate_total = lax.dot_general(token_rows, pregate, over_rows, preferred_element_type=F32)
    up_total = lax.dot_general(token_rows, preup, over_rows, preferred_element_type=F32)

    grad_tokens, grad_gates = combine(expert_ids, pair_slot, gate_weights, back_packed, width)
    return (
        grad_tokens,
        grad_gates.T,
        gate_total[None].astype(BF16),
        up_total[None].astype(BF16),
        down_total[None].astype(BF16),
    )


def solution(mesh):
    rows = P(AXES, None)
    blocks = P(AXES, None, None)
    return jax.shard_map(
        body,
        mesh=mesh,
        in_specs=(rows,) * 5 + (blocks,) * 5,
        out_specs=(rows, rows, blocks, blocks, blocks),
        check_vma=False,
    )
```

```python
import functools

import jax
import jax.numpy as jnp
from jax import lax
from jax.experimental import pallas as pl
from jax.experimental.pallas import tpu as pltpu
from jax.sharding import PartitionSpec as P

F32 = jnp.float32
BF16 = jnp.bfloat16
AXES = ("group", "member")
CHUNK = 256
BLOCK = 128
LOAD = 512
NT = (((1,), (1,)), ((), ()))
VMEM_LIMIT = 56 * 1024 * 1024
SMALL_VMEM = 20 * 1024 * 1024

EXTRA = 128


def zero_one(mask):
    return jnp.where(mask, 1.0, 0.0).astype(BF16)


def dot(a, b):
    return jnp.dot(a, b, preferred_element_type=F32)


def packed_ids(index):
    pair, q = index >> 3, index & 7
    return pair * 12 + q, pair * 12 + 8 + (q & 3), q < 4


def side_by_side(a, b):
    lane = lax.broadcasted_iota(jnp.int32, (a.shape[0], EXTRA), 1)
    return jnp.where(lane < EXTRA // 2, a, b).astype(BF16)


def pack_kernel(scaled, ids_ref, slot_ref, gate_ref, x_ref, out_ref, halves_ref, made_ref, sems):
    toks, width = x_ref.shape
    half = width // 2
    rows = BLOCK
    halves_ref[:toks, :] = x_ref[:, :half]
    halves_ref[toks:, :] = x_ref[:, half:]
    dest = ids_ref[...] * 12 + slot_ref[...]
    gate = gate_ref[...].astype(F32) if scaled else jnp.ones(dest.shape, F32)
    copies = []
    for block in range(made_ref.shape[0] // rows):
        index = lax.broadcasted_iota(jnp.int32, (rows, 1), 0) + block * rows
        id_a, id_b, first = packed_ids(index)
        id_low = jnp.where(first, id_b, -1)
        id_high = jnp.where(first, -1, id_b)
        weight_a = jnp.zeros((rows, toks), F32)
        low = jnp.zeros((rows, toks), F32)
        high = jnp.zeros((rows, toks), F32)
        for k in range(dest.shape[0]):
            d, g = dest[k : k + 1, :], gate[k : k + 1, :]
            weight_a = jnp.where(d == id_a, g, weight_a)
            low = jnp.where(d == id_low, g, low)
            high = jnp.where(d == id_high, g, high)
        here = pl.ds(block * rows, rows)
        made_ref[here, :width] = dot(weight_a.astype(BF16), x_ref[...]).astype(BF16)
        made_ref[here, width:] = dot(
            jnp.concatenate([low, high], axis=1).astype(BF16), halves_ref[...]
        ).astype(BF16)
        copy = pltpu.make_async_copy(made_ref.at[here, :], out_ref.at[here, :], sems.at[block])
        copy.start()
        copies.append(copy)
    for copy in copies:
        copy.wait()


def pack(ids_t, slot_t, gates_t, x, packed_rows, scaled):
    toks, width = x.shape
    wide = width * 3 // 2
    return pl.pallas_call(
        functools.partial(pack_kernel, scaled),
        out_specs=pl.BlockSpec(memory_space=pl.ANY),
        out_shape=jax.ShapeDtypeStruct((packed_rows, wide), BF16),
        scratch_shapes=[
            pltpu.VMEM((2 * toks, width // 2), BF16),
            pltpu.VMEM((packed_rows, wide), BF16),
            pltpu.SemaphoreType.DMA((packed_rows // BLOCK,)),
        ],
        compiler_params=pltpu.CompilerParams(vmem_limit_bytes=VMEM_LIMIT),
        cost_estimate=pl.CostEstimate(
            flops=2 * packed_rows * toks * width * 2,
            bytes_accessed=packed_rows * width * 3,
            transcendentals=0,
        ),
    )(ids_t, slot_t, gates_t, x)


def sort_kernel(a_ref, b_ref, out_a, out_b):
    rows = a_ref.shape[0]
    n = lax.broadcasted_iota(jnp.int32, (rows, rows), 0)
    col = lax.broadcasted_iota(jnp.int32, (rows, rows), 1)
    cut = rows * 2 // 3
    m = n - cut
    source = jnp.where(n < cut, (n >> 3) * 12 + (n & 7), (m >> 2) * 12 + 8 + (m & 3))
    perm = zero_one(col == source)
    out_a[...] = dot(perm, a_ref[...]).astype(BF16)
    out_b[...] = dot(perm, b_ref[...]).astype(BF16)


def sort_rows(a, b):
    rows, width = a.shape
    step = CHUNK * 3 // 2
    spec = pl.BlockSpec((step, width), lambda i: (i, 0))
    return pl.pallas_call(
        sort_kernel,
        grid=(rows // step,),
        in_specs=[spec, spec],
        out_specs=[spec, spec],
        out_shape=[jax.ShapeDtypeStruct((rows, width), BF16)] * 2,
        compiler_params=pltpu.CompilerParams(vmem_limit_bytes=VMEM_LIMIT),
        cost_estimate=pl.CostEstimate(
            flops=4 * rows * step * width, bytes_accessed=rows * width * 8, transcendentals=0
        ),
    )(a, b)


def fold_masks(out_rows, in_rows):
    n = lax.broadcasted_iota(jnp.int32, (out_rows, in_rows), 0)
    p = lax.broadcasted_iota(jnp.int32, (out_rows, in_rows), 1)
    low = (n >> 2) * 8 + (n & 3)
    return zero_one(p == low), zero_one(p == low + 4)


def unpack_into(packed_ref, rows_ref):
    packed = packed_ref.shape[0]
    width = rows_ref.shape[1]
    half = width // 2
    rows_ref[:packed, :] = packed_ref[:, :width]
    low, high = fold_masks(packed // 2, packed)
    rest = packed_ref[:, width : width + half]
    rows_ref[packed:, :half] = dot(low, rest).astype(BF16)
    rows_ref[packed:, half:] = dot(high, rest).astype(BF16)


def unpack(packed):
    total, wide = packed.shape
    width = wide * 2 // 3
    return pl.pallas_call(
        unpack_into,
        grid=(total // CHUNK,),
        in_specs=[pl.BlockSpec((CHUNK, wide), lambda i: (i, 0))],
        out_specs=pl.BlockSpec((CHUNK * 3 // 2, width), lambda i: (i, 0)),
        out_shape=jax.ShapeDtypeStruct((total * 3 // 2, width), BF16),
        compiler_params=pltpu.CompilerParams(vmem_limit_bytes=SMALL_VMEM),
        cost_estimate=pl.CostEstimate(
            flops=total * CHUNK * width * 2, bytes_accessed=total * wide * 4, transcendentals=0
        ),
    )(packed)


def expert_kernel(
    packed_ref,
    a_ref,
    b_ref,
    wg_ref,
    wu_ref,
    wd_ref,
    back_ref,
    rows_ref,
    hidden_ref,
    pregate_ref,
    preup_ref,
):
    packed = packed_ref.shape[0]
    width = rows_ref.shape[1]
    half = width // 2
    unpack_into(packed_ref, rows_ref)
    back_hidden = lax.dot_general(rows_ref[...], wd_ref[...], NT, preferred_element_type=F32)
    a = a_ref[...].astype(F32)
    b = b_ref[...].astype(F32)
    sig = jax.nn.sigmoid(a)
    swish = a * sig
    hidden = swish * b
    hidden_ref[...] = hidden.astype(BF16)
    slot_gate = jnp.sum(hidden * back_hidden, axis=1, keepdims=True).astype(BF16)
    pregate = (back_hidden * b * sig * (1.0 + a * (1.0 - sig))).astype(BF16)
    preup = (back_hidden * swish).astype(BF16)
    pregate_ref[...] = pregate
    preup_ref[...] = preup
    slot_grad = (
        lax.dot_general(pregate, wg_ref[...], NT, preferred_element_type=F32)
        + lax.dot_general(preup, wu_ref[...], NT, preferred_element_type=F32)
    ).astype(BF16)
    back_ref[:, :width] = slot_grad[:packed, :]
    p = lax.broadcasted_iota(jnp.int32, (packed, packed // 2), 0)
    n = lax.broadcasted_iota(jnp.int32, (packed, packed // 2), 1)
    same = n == (p >> 3) * 4 + (p & 3)
    first = (p & 7) < 4
    rest = slot_grad[packed:, :]
    back_ref[:, width : width + half] = (
        dot(zero_one(same & first), rest[:, :half])
        + dot(zero_one(same & jnp.logical_not(first)), rest[:, half:])
    ).astype(BF16)
    last = jnp.broadcast_to(slot_gate[packed:, :], (packed // 2, EXTRA))
    back_ref[:, width + half :] = side_by_side(
        slot_gate[:packed, :].astype(F32), dot(zero_one(same), last)
    )


def expert(packed, a, b, weight_gate, weight_up, weight_down):
    total, wide = packed.shape
    rows = a.shape[0]
    hidden_units, width = weight_down.shape
    step = CHUNK * 3 // 2
    narrow = pl.BlockSpec((step, hidden_units), lambda i: (i, 0))
    packed_spec = pl.BlockSpec((CHUNK, wide), lambda i: (i, 0))
    back_spec = pl.BlockSpec((CHUNK, wide + EXTRA), lambda i: (i, 0))
    return pl.pallas_call(
        expert_kernel,
        grid=(total // CHUNK,),
        in_specs=[
            packed_spec,
            narrow,
            narrow,
            pl.BlockSpec(weight_gate.shape, lambda i: (0, 0)),
            pl.BlockSpec(weight_up.shape, lambda i: (0, 0)),
            pl.BlockSpec(weight_down.shape, lambda i: (0, 0)),
        ],
        out_specs=[
            back_spec,
            pl.BlockSpec((step, width), lambda i: (i, 0)),
            narrow,
            narrow,
            narrow,
        ],
        out_shape=[
            jax.ShapeDtypeStruct((total, wide + EXTRA), BF16),
            jax.ShapeDtypeStruct((rows, width), BF16),
            jax.ShapeDtypeStruct((rows, hidden_units), BF16),
            jax.ShapeDtypeStruct((rows, hidden_units), BF16),
            jax.ShapeDtypeStruct((rows, hidden_units), BF16),
        ],
        compiler_params=pltpu.CompilerParams(vmem_limit_bytes=VMEM_LIMIT),
        cost_estimate=pl.CostEstimate(
            flops=6 * rows * width * hidden_units,
            bytes_accessed=total * wide * 6,
            transcendentals=rows * hidden_units,
        ),
    )(packed, a, b, weight_gate, weight_up, weight_down)


def combine_kernel(
    ids_ref, slot_ref, gate_ref, packed_ref, out_ref, terms_ref, here_ref, masks_ref, sems
):
    toks, width = out_ref.shape
    half = width // 2
    total = here_ref.shape[0]
    rows = LOAD
    copies = []
    for block in range(total // rows):
        at = pl.ds(block * rows, rows)
        copy = pltpu.make_async_copy(packed_ref.at[at, :], here_ref.at[at, :], sems.at[block])
        copy.start()
        copies.append(copy)

    ids = ids_ref[...]
    dest = ids * 12 + slot_ref[...]
    columns = [jnp.broadcast_to(dest[:, k : k + 1], (toks, 128)) for k in range(dest.shape[1])]
    for start in range(0, total, 128):
        index = lax.broadcasted_iota(jnp.int32, (1, 128), 1) + start
        id_a, id_b, first = packed_ids(index)
        id_low = jnp.where(first, id_b, -1)
        id_high = jnp.where(first, -1, id_b)
        hits = [column == id_a for column in columns]
        lows = [column == id_low for column in columns]
        highs = [column == id_high for column in columns]
        for n, found in enumerate((hits, lows, highs)):
            mask = functools.reduce(jnp.logical_or, found)
            masks_ref[n * toks : (n + 1) * toks, start : start + 128] = zero_one(mask)

    terms = jnp.zeros((toks, EXTRA), F32)
    left = jnp.zeros((toks, half), F32)
    right = jnp.zeros((toks, half), F32)
    for block, copy in enumerate(copies):
        copy.wait()
        at = slice(block * rows, (block + 1) * rows)
        one_a = masks_ref[:toks, at]
        folded = dot(masks_ref[toks:, at], here_ref[at, width : width + half])
        left += dot(one_a, here_ref[at, :half]) + folded[:toks, :]
        right += dot(one_a, here_ref[at, half:width]) + folded[toks:, :]
        extra = here_ref[at, width + half :]
        lane = lax.broadcasted_iota(jnp.int32, (rows, EXTRA), 1)
        pair = (lax.broadcasted_iota(jnp.int32, (rows, EXTRA), 0) + block * rows) >> 3
        zero = jnp.zeros((), BF16)
        value_a = jnp.where(lane == pair, extra[:, :1], zero)
        value_b = jnp.where(lane == pair, extra[:, EXTRA // 2 : EXTRA // 2 + 1], zero)
        terms += dot(one_a, value_a) + dot(masks_ref[toks : 2 * toks, at], value_b)
    out_ref[:, :half] = left.astype(BF16)
    out_ref[:, half:] = right.astype(BF16)

    expert_lane = lax.broadcasted_iota(jnp.int32, terms.shape, 1)
    found = jnp.zeros(terms.shape, F32)
    for k in range(ids.shape[1]):
        mine = jnp.where(expert_lane == ids[:, k : k + 1], terms, 0.0)
        term = jnp.sum(mine, axis=1, keepdims=True) / gate_ref[:, k : k + 1].astype(F32)
        found = jnp.where(expert_lane == k, term, found)
    row = lax.broadcasted_iota(jnp.int32, (16, EXTRA), 0)
    column = lax.broadcasted_iota(jnp.int32, (16, EXTRA), 1)
    turned = lax.dot_general(
        zero_one(column == row), found.astype(BF16), NT, preferred_element_type=F32
    )
    terms_ref[...] = turned[: terms_ref.shape[0], :].astype(BF16)


def combine(ids, slots, gates, packed, width):
    toks, routes = ids.shape
    total, wide = packed.shape
    table = pl.BlockSpec(memory_space=pltpu.VMEM)
    return pl.pallas_call(
        combine_kernel,
        in_specs=[table, table, table, pl.BlockSpec(memory_space=pl.ANY)],
        out_shape=[
            jax.ShapeDtypeStruct((toks, width), BF16),
            jax.ShapeDtypeStruct((routes, toks), BF16),
        ],
        scratch_shapes=[
            pltpu.VMEM((total, wide), BF16),
            pltpu.VMEM((3 * toks, total), BF16),
            pltpu.SemaphoreType.DMA((total // LOAD,)),
        ],
        compiler_params=pltpu.CompilerParams(vmem_limit_bytes=SMALL_VMEM),
        cost_estimate=pl.CostEstimate(
            flops=2 * total * toks * width * 2, bytes_accessed=total * wide * 2, transcendentals=0
        ),
    )(ids, slots, gates, packed)


def exchange(x, axes):
    return lax.all_to_all(x, axes, split_axis=0, concat_axis=0, tiled=True)


def body(
    tokens,
    grad_out,
    expert_ids,
    pair_slot,
    gate_weights,
    weight_gate,
    weight_up,
    weight_down,
    saved_gate,
    saved_up,
):
    experts = lax.axis_size("group") * lax.axis_size("member")
    width = tokens.shape[1]
    packed_rows = experts * 8
    routing = (expert_ids.T, pair_slot.T, gate_weights.T)

    here_grads = exchange(pack(*routing, grad_out, packed_rows, True), AXES)
    here_tokens = exchange(pack(*routing, tokens, packed_rows, False), AXES)
    a, b = sort_rows(saved_gate[0], saved_up[0])
    back, grad_rows, hidden, pregate, preup = expert(
        here_grads, a, b, weight_gate[0], weight_up[0], weight_down[0]
    )
    back, here_tokens = lax.optimization_barrier((back, here_tokens))
    back_packed = exchange(back, AXES)

    token_rows = unpack(here_tokens)
    over_rows = (((0,), (0,)), ((), ()))
    down_total = lax.dot_general(hidden, grad_rows, over_rows, preferred_element_type=F32)
    gate_total = lax.dot_general(token_rows, pregate, over_rows, preferred_element_type=F32)
    up_total = lax.dot_general(token_rows, preup, over_rows, preferred_element_type=F32)

    grad_tokens, grad_gates = combine(expert_ids, pair_slot, gate_weights, back_packed, width)
    return (
        grad_tokens,
        grad_gates.T,
        gate_total[None].astype(BF16),
        up_total[None].astype(BF16),
        down_total[None].astype(BF16),
    )


def solution(mesh):
    rows = P(AXES, None)
    blocks = P(AXES, None, None)
    return jax.shard_map(
        body,
        mesh=mesh,
        in_specs=(rows,) * 5 + (blocks,) * 5,
        out_specs=(rows, rows, blocks, blocks, blocks),
        check_vma=False,
    )
```
